1024 devices in a mesh: ctx: 128 (over x, z, core), head: 8 (over y).
Axes of the slice: x: 4, y: 8, z: 16, core: 2. Of those that a mesh axis runs over, the one named last changes fastest.
Arguments:
- queries: bfloat16 [16384, 6144], P('ctx', 'head'), may hold values from -6 to 6
- key_input: bfloat16 [16384, 6144], P('ctx', 'head'), may hold values from -6 to 6
- value_input: bfloat16 [16384, 6144], P('ctx', 'head'), may hold values from -6 to 6
- norm_gain: float32 [6144], P('head'), may hold values from 0.5 to 1.5
- cotangent: bfloat16 [16384, 6144], P('ctx', 'head'), may hold values from -6 to 6
Outputs:
- attended: bfloat16 [16384, 6144], P('ctx', 'head')
- grad_query: bfloat16 [16384, 6144], P('ctx', 'head')
- grad_key: bfloat16 [16384, 6144], P('ctx', 'head')
- grad_value: bfloat16 [16384, 6144], P('ctx', 'head')
The draws below stay inside these ranges and needn't reach their ends.
All inputs are finite; a program needn't handle non-finite values.
Results may differ from the reference program's by a relative error of at most 0.0065.
Values sent between devices are 32-bit elements; how exact they have to be, the bound alone decides.
No kernel may reach another device: no remote copies, remote signals or barrier semaphores. Data moves between devices by JAX's collectives and lax.ppermute only.
A program may use at most 128 MiB of HBM per device.

```python
import jax
import jax.numpy as jnp
from jax import lax

HEADS = 64
HEAD_DIM = 96
D = 6144
TOK_DEV = 128
TOKENS = 16384
N_CTX = 128


def levels(rng, extent, split, least, top_value):
    level, own = 1.0, jax.random.fold_in(rng, 6)
    for axis_at, shards_of in split:
        steps = jnp.exp(jax.random.uniform(jax.random.fold_in(own, axis_at), (shards_of,), jnp.float32, least / len(split), top_value / len(split)))
        level = level * jnp.repeat(steps, extent[axis_at] // shards_of).reshape([-1 if axis == axis_at else 1 for axis in range(len(extent))])
    return level


def scatter_about(stream_key, shape, scale, limit, pieces=(), kind=jnp.bfloat16):
    values = scale * jax.random.normal(stream_key, shape, jnp.float32)
    if pieces:
        values = values * levels(stream_key, shape, pieces, -0.22, 0.18)
    return jnp.clip(values, -limit, limit).astype(kind)


def setup_inputs(seed: int = 0) -> dict:
    streams_of = jax.random.split(jax.random.key(seed), 6)
    queries = scatter_about(streams_of[0], (TOKENS, D), 1.0, 6.0, ((0, 128), (1, 8)))
    key_input = scatter_about(streams_of[1], (TOKENS, D), 1.0, 6.0, ((0, 128), (1, 8)))
    value_input = scatter_about(streams_of[2], (TOKENS, D), 1.0, 6.0, ((0, 128), (1, 8)))
    norm_gain = jnp.clip(1.0 + 0.1 * jax.random.normal(streams_of[3], (D,), jnp.float32), 0.5, 1.5)
    cotangent = scatter_about(streams_of[4], (TOKENS, D), 1.0, 6.0, ((0, 128), (1, 8)))
    return dict(queries=queries, key_input=key_input, value_input=value_input, norm_gain=norm_gain, cotangent=cotangent)


epsilon = 1e-06

def lowered(x):
    return lax.optimization_barrier(x.astype(jnp.bfloat16)).astype(jnp.float32)

def silu_slope(x):
    sig = jax.nn.sigmoid(x)
    return sig * (1.0 + x * (1.0 - sig))

def reference(queries, key_input, value_input, norm_gain, cotangent):
    blocks = N_CTX
    shape3 = (TOK_DEV, HEADS, HEAD_DIM)
    q_blocks = queries.reshape(blocks, TOK_DEV, D)
    k_blocks = key_input.reshape(blocks, TOK_DEV, D)
    v_blocks = value_input.reshape(blocks, TOK_DEV, D)
    c_blocks = cotangent.reshape(blocks, TOK_DEV, D)
    gain = norm_gain.astype(jnp.float32)
    causal = jnp.arange(TOK_DEV)[:, None] >= jnp.arange(TOK_DEV)[None, :]
    zeros = jnp.zeros((HEADS, HEAD_DIM, HEAD_DIM), jnp.float32)

    def forward(prefix, block):
        k_blk, v_blk = block
        k_feat = lowered(jax.nn.silu(k_blk.astype(jnp.float32))).reshape(shape3)
        values = v_blk.astype(jnp.float32).reshape(shape3)
        return (prefix + jnp.einsum('shd,she->hde', k_feat, values), lowered(prefix))
    last_state, prefixes = lax.scan(forward, zeros, (k_blocks, v_blocks))

    def backward(later, block):
        q_blk, k_blk, v_blk, c_blk, pre_low = block
        q_float = q_blk.astype(jnp.float32)
        k_float = k_blk.astype(jnp.float32)
        q_feat = lowered(jax.nn.silu(q_float)).reshape(shape3)
        k_feat = lowered(jax.nn.silu(k_float)).reshape(shape3)
        values = v_blk.astype(jnp.float32).reshape(shape3)
        attn = lowered(jnp.where(causal[None], jnp.einsum('thd,shd->hts', q_feat, k_feat), 0.0))
        raw = jnp.einsum('hts,shd->thd', attn, values) + jnp.einsum('thd,hde->the', q_feat, pre_low)
        raw = raw.reshape(TOK_DEV, D)
        rms = jnp.sqrt(lax.optimization_barrier(jnp.sum(raw * raw, axis=1)) / D + epsilon)
        attended = (raw / rms[:, None] * gain[None, :]).astype(jnp.bfloat16)
        upstream = c_blk.astype(jnp.float32) * gain[None, :]
        cross = lax.optimization_barrier(jnp.sum(upstream * raw, axis=1))
        d_raw = lowered((upstream - raw * (cross / (D * rms * rms))[:, None]) / rms[:, None]).reshape(shape3)
        back = lowered(jnp.where(causal[None], jnp.einsum('the,she->hts', d_raw, values), 0.0))
        later_low = lowered(later)
        grad_qf = jnp.einsum('hts,shd->thd', back, k_feat) + jnp.einsum('the,hde->thd', d_raw, pre_low)
        grad_kf = jnp.einsum('hts,thd->shd', back, q_feat) + jnp.einsum('she,hde->shd', values, later_low)
        grad_v = jnp.einsum('hts,the->she', attn, d_raw) + jnp.einsum('shd,hde->she', k_feat, later_low)
        grad_q = (grad_qf.reshape(TOK_DEV, D) * silu_slope(q_float)).astype(jnp.bfloat16)
        grad_k = (grad_kf.reshape(TOK_DEV, D) * silu_slope(k_float)).astype(jnp.bfloat16)
        grad_v = grad_v.reshape(TOK_DEV, D).astype(jnp.bfloat16)
        return (later + jnp.einsum('thd,the->hde', q_feat, d_raw), (attended, grad_q, grad_k, grad_v))
    first_later, outs = lax.scan(backward, zeros, (q_blocks, k_blocks, v_blocks, c_blocks, prefixes), reverse=True)
    attended, grad_q, grad_k, grad_v = outs
    return (attended.reshape(TOKENS, D), grad_q.reshape(TOKENS, D), grad_k.reshape(TOKENS, D), grad_v.reshape(TOKENS, D))
```

```python
import jax
import jax.numpy as jnp
from jax import lax
from jax.experimental import pallas as pl
from jax.sharding import PartitionSpec as P

HEAD_DIM = 96
D = 6144
CHIPS = 64
CORES = 2

epsilon = 1e-06


def swap_cores(x):
    pairs = [(i, i ^ 1) for i in range(CHIPS * CORES)]
    return lax.ppermute(x, "ctx", pairs)


def across_chips(x):
    groups = [[chip * CORES + core for chip in range(CHIPS)] for core in range(CORES)]
    return lax.all_to_all(x, "ctx", 0, 0, axis_index_groups=groups)


def rounded(here_ref, there_ref, out_ref):
    core = lax.axis_index("ctx") % CORES
    here, there = here_ref[...], there_ref[...]
    out_ref[0] = jnp.where(core == 0, here, there).astype(jnp.bfloat16)
    out_ref[1] = jnp.where(core == 0, there, here).astype(jnp.bfloat16)


def exclusive(state, backward):
    core = lax.axis_index("ctx") % CORES
    halves = state.reshape(CORES, CHIPS, -1)
    mine = lax.dynamic_index_in_dim(halves, core, 0, False)
    theirs = lax.dynamic_index_in_dim(halves, 1 - core, 0, False)
    received = swap_cores(theirs)
    pieces = across_chips((mine + received)[:, None, :])[:, 0, :]
    order = jnp.arange(CHIPS)
    if backward:
        before = order[:, None] < order[None, :]
        first = core == 1
    else:
        before = order[:, None] > order[None, :]
        first = core == 0
    summed = jnp.dot(before.astype(jnp.float32), pieces, precision=lax.Precision.HIGHEST)
    chip = across_chips(summed[:, None, :])[:, 0, :]
    zero = jnp.zeros_like(mine)
    here = chip + jnp.where(first, zero, received)
    there = swap_cores(chip + jnp.where(first, mine, zero))
    low = pl.pallas_call(
        rounded, out_shape=jax.ShapeDtypeStruct((CORES,) + here.shape, jnp.bfloat16)
    )(here, there)
    return low.reshape(state.shape)


def silu_slope(x):
    sig = jax.nn.sigmoid(x)
    return sig * (1.0 + x * (1.0 - sig))


def per_device(queries, key_input, value_input, norm_gain, cotangent):
    tok_rows = queries.shape[0]
    heads_here = queries.shape[1] // HEAD_DIM
    shape3 = (tok_rows, heads_here, HEAD_DIM)
    q_float = queries.astype(jnp.float32)
    k_float = key_input.astype(jnp.float32)
    q_feat = jax.nn.silu(q_float).astype(jnp.bfloat16).reshape(shape3)
    k_feat = jax.nn.silu(k_float).astype(jnp.bfloat16).reshape(shape3)
    values = value_input.reshape(shape3)
    causal = jnp.arange(tok_rows)[:, None] >= jnp.arange(tok_rows)[None, :]
    local_state = jnp.einsum("shd,she->hde", k_feat, values, preferred_element_type=jnp.float32)
    prefix_low = exclusive(local_state, False)
    scores = jnp.einsum("thd,shd->hts", q_feat, k_feat, preferred_element_type=jnp.float32)
    attn_low = jnp.where(causal[None], scores, 0.0).astype(jnp.bfloat16)
    raw = jnp.einsum("hts,shd->thd", attn_low, values, preferred_element_type=jnp.float32)
    raw = raw + jnp.einsum("thd,hde->the", q_feat, prefix_low, preferred_element_type=jnp.float32)
    raw = raw.reshape(tok_rows, heads_here * HEAD_DIM)
    upstream = cotangent.astype(jnp.float32) * norm_gain[None, :]
    parts = jnp.stack([jnp.sum(raw * raw, axis=1), jnp.sum(upstream * raw, axis=1)])
    parts = jnp.broadcast_to(parts[None], (8,) + parts.shape)
    totals = jnp.sum(lax.all_to_all(parts, "head", 0, 0), axis=0)
    square_total, cross_total = totals[0], totals[1]
    rms = jnp.sqrt(square_total / D + epsilon)
    attended = (raw / rms[:, None] * norm_gain[None, :]).astype(jnp.bfloat16)
    d_raw = (upstream - raw * (cross_total / (D * rms * rms))[:, None]) / rms[:, None]
    d_raw = d_raw.astype(jnp.bfloat16).reshape(shape3)
    local_grad = jnp.einsum("thd,the->hde", q_feat, d_raw, preferred_element_type=jnp.float32)
    later_low = exclusive(local_grad, True)
    back = jnp.einsum("the,she->hts", d_raw, values, preferred_element_type=jnp.float32)
    back_low = jnp.where(causal[None], back, 0.0).astype(jnp.bfloat16)
    grad_qf = jnp.einsum("hts,shd->thd", back_low, k_feat, preferred_element_type=jnp.float32)
    grad_qf = grad_qf + jnp.einsum(
        "the,hde->thd", d_raw, prefix_low, preferred_element_type=jnp.float32
    )
    grad_kf = jnp.einsum("hts,thd->shd", back_low, q_feat, preferred_element_type=jnp.float32)
    grad_kf = grad_kf + jnp.einsum(
        "she,hde->shd", values, later_low, preferred_element_type=jnp.float32
    )
    grad_vf = jnp.einsum("hts,the->she", attn_low, d_raw, preferred_element_type=jnp.float32)
    grad_vf = grad_vf + jnp.einsum(
        "shd,hde->she", k_feat, later_low, preferred_element_type=jnp.float32
    )
    width_here = heads_here * HEAD_DIM
    grad_query = (grad_qf.reshape(tok_rows, width_here) * silu_slope(q_float)).astype(jnp.bfloat16)
    grad_key = (grad_kf.reshape(tok_rows, width_here) * silu_slope(k_float)).astype(jnp.bfloat16)
    grad_value = grad_vf.reshape(tok_rows, width_here).astype(jnp.bfloat16)
    return (attended, grad_query, grad_key, grad_value)


def solution(mesh):
    in_specs = (P("ctx", "head"), P("ctx", "head"), P("ctx", "head"), P("head"), P("ctx", "head"))
    out_specs = (P("ctx", "head"), P("ctx", "head"), P("ctx", "head"), P("ctx", "head"))
    return jax.shard_map(
        per_device, mesh=mesh, in_specs=in_specs, out_specs=out_specs, check_vma=False
    )
```

```python
import jax
import jax.numpy as jnp
from jax import lax
from jax.experimental import pallas as pl
from jax.experimental.pallas import tpu as pltpu
from jax.sharding import PartitionSpec as P

HEAD_DIM = 96
D = 6144
TOK = 128
LANES = 128
HALF_HEADS = 4
HALF = HALF_HEADS * HEAD_DIM
CHIPS = 64
CORES = 2
PIECE = 640

epsilon = 1e-06
F32 = jnp.float32
BF16 = jnp.bfloat16
VMEM = pl.BlockSpec(memory_space=pltpu.VMEM)
NN = (((1,), (0,)), ((), ()))
NT = (((1,), (1,)), ((), ()))
TN = (((0,), (0,)), ((), ()))


def mm(a, b, dims):
    return lax.dot_general(a, b, dims, preferred_element_type=F32)


def half(g):
    return slice(g * HALF, (g + 1) * HALF)


def head_masks(rows):
    lane = lax.broadcasted_iota(jnp.int32, (rows, HALF), 1)
    return [(lane >= h * HEAD_DIM) & (lane < (h + 1) * HEAD_DIM) for h in range(HALF_HEADS)]


def spread(x):
    return jnp.concatenate([x * m.astype(BF16) for m in head_masks(x.shape[0])], axis=0)


def diagonal(x):
    rows = x.shape[0] // HALF_HEADS
    masks = head_masks(rows)
    out = x[:rows]
    for h in range(1, HALF_HEADS):
        out = jnp.where(masks[h], x[h * rows : (h + 1) * rows], out)
    return out


def to_pieces(state):
    rest = state[64:96]
    tail = rest[:, 256:384]
    return jnp.concatenate(
        [
            state[0:64],
            jnp.concatenate([rest[:, 0:128], rest[:, 128:256]], axis=0),
            jnp.concatenate([tail, pltpu.roll(tail, 64, 1)], axis=0),
        ],
        axis=1,
    )


def from_pieces(pieces):
    low = lax.broadcasted_iota(jnp.int32, (32, LANES), 1) < 64
    tail = jnp.where(low, pieces[0:32, 512:640], pltpu.roll(pieces[32:64, 512:640], 64, 1))
    rest = jnp.concatenate([pieces[0:32, 384:512], pieces[32:64, 384:512], tail], axis=1)
    return jnp.concatenate([pieces[:, 0:384], rest], axis=0)


def silu_low(x):
    x = x.astype(F32)
    return (x * jax.nn.sigmoid(x)).astype(BF16)


def silu_slope(x):
    x = x.astype(F32)
    sig = jax.nn.sigmoid(x)
    return sig * (1.0 + x * (1.0 - sig))


def causal4():
    row = lax.broadcasted_iota(jnp.int32, (TOK, TOK), 0)
    col = lax.broadcasted_iota(jnp.int32, (TOK, TOK), 1)
    keep = jnp.where(row >= col, 1.0, 0.0)
    return jnp.concatenate([keep] * HALF_HEADS, axis=1) > 0.5


def by_head(x):
    return jnp.concatenate([x[:, h * TOK : (h + 1) * TOK] for h in range(HALF_HEADS)], axis=0)


def store_states(first, second, mine_ref, theirs_ref):
    low = (lax.axis_index("ctx") % CORES) == 0
    first, second = to_pieces(first), to_pieces(second)
    mine_ref[:, 0, :] = jnp.where(low, first, second)
    theirs_ref[:, 0, :] = jnp.where(low, second, first)


def load_states(here_ref, there_ref):
    low = (lax.axis_index("ctx") % CORES) == 0
    here, there = here_ref[:, 0, :], there_ref[:, 0, :]
    pair = jnp.where(low, here, there), jnp.where(low, there, here)
    return [from_pieces(p).astype(BF16) for p in pair]


def state_kernel(k_ref, v_ref, mine_ref, theirs_ref):
    states = [
        diagonal(mm(silu_low(k_ref[:, half(g)]), v_ref[:, half(g)], TN)) for g in range(CORES)
    ]
    store_states(*states, mine_ref, theirs_ref)


def intra_kernel(q_ref, k_ref, v_ref, attn_ref, intra_ref):
    keep = causal4()
    for g in range(CORES):
        q_feat, k_feat = silu_low(q_ref[:, half(g)]), silu_low(k_ref[:, half(g)])
        attn = jnp.where(keep, mm(q_feat, spread(k_feat), NT), 0.0).astype(BF16)
        attn_ref[g] = attn
        intra_ref[:, half(g)] = mm(attn, spread(v_ref[:, half(g)]), NN)


def scan_kernel(backward, pieces_ref, out_ref):
    row = lax.broadcasted_iota(jnp.int32, (CHIPS, CHIPS), 0)
    col = lax.broadcasted_iota(jnp.int32, (CHIPS, CHIPS), 1)
    before = jnp.where(row < col if backward else row > col, 1.0, 0.0)
    out_ref[:, 0, :] = lax.dot_general(
        before, pieces_ref[:, 0, :], NN, precision=lax.Precision.HIGHEST, preferred_element_type=F32
    )


def lane_sums(x):
    part = x[:, 0:LANES]
    for i in range(1, x.shape[1] // LANES):
        part = part + x[:, i * LANES : (i + 1) * LANES]
    return jnp.sum(part.T, axis=0, keepdims=True)


def raw_kernel(q_ref, c_ref, gain_ref, intra_ref, here_ref, there_ref, raw_ref, low_ref, parts_ref):
    for g, state in enumerate(load_states(here_ref, there_ref)):
        low_ref[g] = state
        raw_ref[:, half(g)] = intra_ref[:, half(g)] + mm(
            silu_low(q_ref[:, half(g)]), spread(state), NN
        )
    raw = raw_ref[...]
    upstream = c_ref[...].astype(F32) * gain_ref[...]
    sums = jnp.concatenate([lane_sums(raw * raw), lane_sums(upstream * raw)], axis=0)
    parts_ref[...] = jnp.broadcast_to(sums[None], parts_ref.shape)


def grad_state_kernel(
    q_ref, c_ref, gain_ref, raw_ref, parts_ref, attended_ref, d_raw_ref, mine_ref, theirs_ref
):
    totals = jnp.sum(parts_ref[...], axis=0)
    square = jnp.broadcast_to(totals[0:1], (TOK, LANES)).T
    cross = jnp.broadcast_to(totals[1:2], (TOK, LANES)).T
    mean = square * (1.0 / D) + epsilon
    inverse = lax.rsqrt(mean)
    pull = cross / (D * mean)
    wide = 3
    inverse, pull = (jnp.concatenate([x] * wide, axis=1) for x in (inverse, pull))
    states = []
    for g in range(CORES):
        raw, gain = raw_ref[:, half(g)], gain_ref[:, half(g)]
        attended_ref[:, half(g)] = (raw * inverse * gain).astype(BF16)
        d_raw = ((c_ref[:, half(g)].astype(F32) * gain - raw * pull) * inverse).astype(BF16)
        d_raw_ref[:, half(g)] = d_raw
        states.append(diagonal(mm(silu_low(q_ref[:, half(g)]), d_raw, TN)))
    store_states(*states, mine_ref, theirs_ref)


def back_kernel(
    q_ref, k_ref, v_ref, d_raw_ref, attn_ref, low_ref, grad_q_ref, grad_kf_ref, grad_vf_ref
):
    keep = causal4()
    for g in range(CORES):
        q, d_raw = q_ref[:, half(g)], d_raw_ref[:, half(g)]
        q_feat, k_feat = silu_low(q), silu_low(k_ref[:, half(g)])
        back = jnp.where(keep, mm(d_raw, spread(v_ref[:, half(g)]), NT), 0.0).astype(BF16)
        grad_qf = mm(back, spread(k_feat), NN) + mm(d_raw, spread(low_ref[g]), NT)
        grad_q_ref[:, half(g)] = (grad_qf * silu_slope(q)).astype(BF16)
        grad_kf_ref[:, half(g)] = mm(by_head(back), spread(q_feat), TN)
        grad_vf_ref[:, half(g)] = mm(by_head(attn_ref[g]), spread(d_raw), TN)


def last_kernel(k_ref, v_ref, grad_kf_ref, grad_vf_ref, here_ref, there_ref, grad_k_ref, grad_v_ref):
    for g, state in enumerate(load_states(here_ref, there_ref)):
        k = k_ref[:, half(g)]
        later = spread(state)
        grad_kf = grad_kf_ref[:, half(g)] + mm(v_ref[:, half(g)], later, NT)
        grad_k_ref[:, half(g)] = (grad_kf * silu_slope(k)).astype(BF16)
        grad_vf = grad_vf_ref[:, half(g)] + mm(silu_low(k), later, NN)
        grad_v_ref[:, half(g)] = grad_vf.astype(BF16)


def call(kernel, outs, *args, flops=0):
    return pl.pallas_call(
        kernel,
        out_shape=[jax.ShapeDtypeStruct(shape, kind) for shape, kind in outs],
        in_specs=[VMEM] * len(args),
        out_specs=[VMEM] * len(outs),
        compiler_params=pltpu.CompilerParams(vmem_limit_bytes=32 * 1024 * 1024),
        cost_estimate=pl.CostEstimate(flops=flops, bytes_accessed=1_000_000, transcendentals=0),
    )(*args)


def swap_cores(x):
    pairs = [(i, i ^ 1) for i in range(CHIPS * CORES)]
    return lax.ppermute(x, "ctx", pairs)


def across_chips(x):
    groups = [[chip * CORES + core for chip in range(CHIPS)] for core in range(CORES)]
    return lax.all_to_all(x, "ctx", 0, 0, axis_index_groups=groups)


PIECES = ((CHIPS, 1, PIECE), F32)
WIDE = ((TOK, CORES * HALF), F32)
WIDE_LOW = ((TOK, CORES * HALF), BF16)
ATTN = ((CORES, TOK, HALF_HEADS * TOK), BF16)
STATE_LOW = ((CORES, HEAD_DIM, HALF), BF16)


def exclusive(mine, theirs, backward):
    core = lax.axis_index("ctx") % CORES
    mine_goes = core == (1 if backward else 0)
    received = swap_cores(theirs)
    pieces = across_chips(mine + received)

    def kernel(pieces_ref, out_ref):
        scan_kernel(backward, pieces_ref, out_ref)

    (summed,) = call(kernel, [PIECES], pieces)
    chip = across_chips(summed)
    there = swap_cores(chip + jnp.where(mine_goes, mine, 0.0))
    here = chip + jnp.where(mine_goes, 0.0, received)
    return here, there


def per_device(queries, key_input, value_input, norm_gain, cotangent):
    n_head = lax.axis_size("head")
    gain = norm_gain.reshape(1, -1)
    mine, theirs = call(state_kernel, [PIECES, PIECES], key_input, value_input)
    attn, intra = call(
        intra_kernel, [ATTN, WIDE], queries, key_input, value_input, flops=200_000_000
    )
    here, there = exclusive(mine, theirs, False)
    raw, low, parts = call(
        raw_kernel,
        [WIDE, STATE_LOW, ((n_head, 2, TOK), F32)],
        queries, cotangent, gain, intra, here, there,
    )
    parts = lax.all_to_all(parts, "head", 0, 0)
    attended, d_raw, mine, theirs = call(
        grad_state_kernel,
        [WIDE_LOW, WIDE_LOW, PIECES, PIECES],
        queries, cotangent, gain, raw, parts,
    )
    grad_query, grad_kf, grad_vf = call(
        back_kernel,
        [WIDE_LOW, WIDE, WIDE],
        queries, key_input, value_input, d_raw, attn, low,
        flops=500_000_000,
    )
    here, there = exclusive(mine, theirs, True)
    grad_key, grad_value = call(
        last_kernel,
        [WIDE_LOW, WIDE_LOW],
        key_input, value_input, grad_kf, grad_vf, here, there,
    )
    return (attended, grad_query, grad_key, grad_value)


def solution(mesh):
    in_specs = (P("ctx", "head"), P("ctx", "head"), P("ctx", "head"), P("head"), P("ctx", "head"))
    out_specs = (P("ctx", "head"), P("ctx", "head"), P("ctx", "head"), P("ctx", "head"))
    return jax.shard_map(
        per_device, mesh=mesh, in_specs=in_specs, out_specs=out_specs, check_vma=False
    )
```

```python
import jax
import jax.numpy as jnp
from jax import lax
from jax.experimental import pallas as pl
from jax.experimental.pallas import tpu as pltpu
from jax.sharding import PartitionSpec as P

HEAD_DIM = 96
D = 6144
TOK = 128
LANES = 128
HALF_HEADS = 4
HALF = HALF_HEADS * HEAD_DIM
CHIPS = 64
CORES = 2
PIECE = 640

epsilon = 1e-06
F32 = jnp.float32
BF16 = jnp.bfloat16
VMEM = pl.BlockSpec(memory_space=pltpu.VMEM)
NN = (((1,), (0,)), ((), ()))
NT = (((1,), (1,)), ((), ()))
TN = (((0,), (0,)), ((), ()))


def mm(a, b, dims):
    return lax.dot_general(a, b, dims, preferred_element_type=F32)


def half(g):
    return slice(g * HALF, (g + 1) * HALF)


def head_masks(rows):
    lane = lax.broadcasted_iota(jnp.int32, (rows, HALF), 1)
    return [(lane >= h * HEAD_DIM) & (lane < (h + 1) * HEAD_DIM) for h in range(HALF_HEADS)]


def spread(x):
    return jnp.concatenate([x * m.astype(BF16) for m in head_masks(x.shape[0])], axis=0)


def diagonal(x):
    rows = x.shape[0] // HALF_HEADS
    masks = head_masks(rows)
    out = x[:rows]
    for h in range(1, HALF_HEADS):
        out = jnp.where(masks[h], x[h * rows : (h + 1) * rows], out)
    return out


def to_pieces(state):
    rest = state[64:96]
    tail = rest[:, 256:384]
    return jnp.concatenate(
        [
            state[0:64],
            jnp.concatenate([rest[:, 0:128], rest[:, 128:256]], axis=0),
            jnp.concatenate([tail, pltpu.roll(tail, 64, 1)], axis=0),
        ],
        axis=1,
    )


def from_pieces(pieces):
    low = lax.broadcasted_iota(jnp.int32, (32, LANES), 1) < 64
    tail = jnp.where(low, pieces[0:32, 512:640], pltpu.roll(pieces[32:64, 512:640], 64, 1))
    rest = jnp.concatenate([pieces[0:32, 384:512], pieces[32:64, 384:512], tail], axis=1)
    return jnp.concatenate([pieces[:, 0:384], rest], axis=0)


def silu_low(x):
    x = x.astype(F32)
    return (x * jax.nn.sigmoid(x)).astype(BF16)


def silu_slope(x):
    x = x.astype(F32)
    sig = jax.nn.sigmoid(x)
    return sig * (1.0 + x * (1.0 - sig))


def causal4():
    row = lax.broadcasted_iota(jnp.int32, (TOK, TOK), 0)
    col = lax.broadcasted_iota(jnp.int32, (TOK, TOK), 1)
    keep = jnp.where(row >= col, 1.0, 0.0)
    return jnp.concatenate([keep] * HALF_HEADS, axis=1) > 0.5


def by_head(x):
    return jnp.concatenate([x[:, h * TOK : (h + 1) * TOK] for h in range(HALF_HEADS)], axis=0)


def core_index():
    return lax.axis_index("ctx") % CORES


def pick(own, x):
    first = (core_index() == 0) == own
    return jnp.where(first, x[:, half(0)], x[:, half(1)])


def in_order(own, other):
    first = core_index() == 0
    return jnp.where(first, own, other), jnp.where(first, other, own)


def state_kernel(k_ref, v_ref, mine_ref, theirs_ref):
    first, second = (
        to_pieces(diagonal(mm(silu_low(k_ref[:, half(g)]), v_ref[:, half(g)], TN)))
        for g in range(CORES)
    )
    low = core_index() == 0
    mine_ref[:, 0, :] = jnp.where(low, first, second)
    theirs_ref[:, 0, :] = jnp.where(low, second, first)


def send_kernel(q_ref, k_ref, v_ref, c_ref, out_ref):
    for i, ref in enumerate((q_ref, k_ref, v_ref, c_ref)):
        out_ref[i] = pick(False, ref[...]).astype(F32)


def attention(q_feat, k_feat):
    return jnp.where(causal4(), mm(q_feat, spread(k_feat), NT), 0.0).astype(BF16)


def intra_kernel(q_ref, k_ref, v_ref, got_ref, intra_ref):
    mine = [pick(True, ref[...]) for ref in (q_ref, k_ref, v_ref)]
    others = [got_ref[i].astype(BF16) for i in range(3)]
    for i, (q, k, v) in enumerate((mine, others)):
        intra_ref[i] = mm(attention(silu_low(q), silu_low(k)), spread(v), NN)


def scan_kernel(backward, pieces_ref, out_ref):
    row = lax.broadcasted_iota(jnp.int32, (CHIPS, CHIPS), 0)
    col = lax.broadcasted_iota(jnp.int32, (CHIPS, CHIPS), 1)
    before = jnp.where(row < col if backward else row > col, 1.0, 0.0)
    out_ref[:, 0, :] = lax.dot_general(
        before, pieces_ref[:, 0, :], NN, precision=lax.Precision.HIGHEST, preferred_element_type=F32
    )


def lane_sums(x):
    part = x[:, 0:LANES]
    for i in range(1, x.shape[1] // LANES):
        part = part + x[:, i * LANES : (i + 1) * LANES]
    return jnp.sum(part.T, axis=0, keepdims=True)


def raw_kernel(
    q_ref, c_ref, gain_ref, got_ref, intra_ref, chip_ref, mine_ref, received_ref,
    raw_ref, low_ref, give_ref, parts_ref,
):
    core = core_index()
    chip = chip_ref[:, 0, :]
    own = from_pieces(chip + jnp.where(core == 1, received_ref[:, 0, :], 0.0))
    other = from_pieces(chip + jnp.where(core == 0, mine_ref[:, 0, :], 0.0))
    low_ref[...] = own.astype(BF16)
    give_ref[TOK:, :] = other
    gain = pick(True, gain_ref[...])
    q, c = pick(True, q_ref[...]), pick(True, c_ref[...])
    sums = []
    for i, (q, c, state) in enumerate(
        ((q, c, own), (got_ref[0].astype(BF16), got_ref[3], other))
    ):
        raw = intra_ref[i] + mm(silu_low(q), spread(state.astype(BF16)), NN)
        raw_ref[i] = raw
        upstream = c.astype(F32) * gain
        sums.append(jnp.concatenate([lane_sums(raw * raw), lane_sums(upstream * raw)], axis=0))
    give_ref[0:TOK, :] = raw_ref[1]
    sums = jnp.concatenate(in_order(*sums), axis=0)
    parts_ref[...] = jnp.broadcast_to(sums[None], parts_ref.shape)


def scales(totals):
    square = jnp.broadcast_to(totals[0:1], (TOK, LANES)).T
    cross = jnp.broadcast_to(totals[1:2], (TOK, LANES)).T
    mean = square * (1.0 / D) + epsilon
    pair = lax.rsqrt(mean), cross / (D * mean)
    return [jnp.concatenate([x] * (HALF // LANES), axis=1) for x in pair]


def gradient(c, gain, raw, inverse, pull):
    return ((c.astype(F32) * gain - raw * pull) * inverse).astype(BF16)


def own_and_other(parts_ref):
    totals = jnp.sum(parts_ref[...], axis=0)
    return in_order(totals[0:2], totals[2:4])


def grad_state_kernel(
    q_ref, c_ref, gain_ref, got_ref, raw_ref, parts_ref, sum_ref, here_ref, there_ref
):
    core = core_index()
    gain = pick(True, gain_ref[...])
    q, c = pick(True, q_ref[...]), pick(True, c_ref[...])
    states = []
    for i, (q, c, totals) in enumerate(
        zip((q, got_ref[0].astype(BF16)), (c, got_ref[3]), own_and_other(parts_ref))
    ):
        d_raw = gradient(c, gain, raw_ref[i], *scales(totals))
        states.append(to_pieces(diagonal(mm(silu_low(q), d_raw, TN))))
    sum_ref[:, 0, :] = states[0] + states[1]
    here_ref[:, 0, :] = jnp.where(core == 0, states[1], 0.0)
    there_ref[:, 0, :] = jnp.where(core == 1, states[0], 0.0)


def back_kernel(
    q_ref, k_ref, v_ref, c_ref, gain_ref, raw_ref, low_ref, got_ref, parts_ref,
    attended_ref, grad_q_ref, grad_kf_ref, grad_vf_ref,
):
    keep = causal4()
    inverse, pull = scales(own_and_other(parts_ref)[0])
    raws = in_order(raw_ref[0], got_ref[0:TOK])
    lows = in_order(low_ref[...].astype(F32), got_ref[TOK:])
    for g in range(CORES):
        q, raw, gain = q_ref[:, half(g)], raws[g], gain_ref[:, half(g)]
        q_feat, k_feat = silu_low(q), silu_low(k_ref[:, half(g)])
        attended_ref[:, half(g)] = (raw * inverse * gain).astype(BF16)
        d_raw = gradient(c_ref[:, half(g)], gain, raw, inverse, pull)
        back = jnp.where(keep, mm(d_raw, spread(v_ref[:, half(g)]), NT), 0.0).astype(BF16)
        grad_qf = mm(back, spread(k_feat), NN) + mm(d_raw, spread(lows[g].astype(BF16)), NT)
        grad_q_ref[:, half(g)] = (grad_qf * silu_slope(q)).astype(BF16)
        grad_kf_ref[:, half(g)] = mm(by_head(back), spread(q_feat), TN)
        grad_vf_ref[:, half(g)] = mm(by_head(attention(q_feat, k_feat)), spread(d_raw), TN)


def last_kernel(
    k_ref, v_ref, grad_kf_ref, grad_vf_ref, chip_ref, here_ref, there_ref, grad_k_ref, grad_v_ref
):
    states = in_order(chip_ref[:, 0, :] + here_ref[:, 0, :], there_ref[:, 0, :])
    for g, state in enumerate(states):
        k = k_ref[:, half(g)]
        later = spread(from_pieces(state).astype(BF16))
        grad_kf = grad_kf_ref[:, half(g)] + mm(v_ref[:, half(g)], later, NT)
        grad_k_ref[:, half(g)] = (grad_kf * silu_slope(k)).astype(BF16)
        grad_vf = grad_vf_ref[:, half(g)] + mm(silu_low(k), later, NN)
        grad_v_ref[:, half(g)] = grad_vf.astype(BF16)


def call(kernel, outs, *args, flops=0):
    return pl.pallas_call(
        kernel,
        out_shape=[jax.ShapeDtypeStruct(shape, kind) for shape, kind in outs],
        in_specs=[VMEM] * len(args),
        out_specs=[VMEM] * len(outs),
        compiler_params=pltpu.CompilerParams(vmem_limit_bytes=32 * 1024 * 1024),
        cost_estimate=pl.CostEstimate(flops=flops, bytes_accessed=1_000_000, transcendentals=0),
    )(*args)


def swap_cores(x):
    pairs = [(i, i ^ 1) for i in range(CHIPS * CORES)]
    return lax.ppermute(x, "ctx", pairs)


def across_chips(x):
    groups = [[chip * CORES + core for chip in range(CHIPS)] for core in range(CORES)]
    return lax.all_to_all(x, "ctx", 0, 0, axis_index_groups=groups)


def over_heads(x):
    size = CORES * lax.axis_size("head")
    groups = [[chip * size + i for i in range(size)] for chip in range(CHIPS)]
    return lax.all_to_all(x, ("ctx", "head"), 0, 0, axis_index_groups=groups)


PIECES = ((CHIPS, 1, PIECE), F32)
WIDE = ((TOK, CORES * HALF), F32)
WIDE_LOW = ((TOK, CORES * HALF), BF16)
BLOCKS = ((CORES, TOK, HALF), F32)


def scan(pieces, backward):
    def kernel(pieces_ref, out_ref):
        scan_kernel(backward, pieces_ref, out_ref)

    (summed,) = call(kernel, [PIECES], across_chips(pieces))
    return across_chips(summed)


def per_device(queries, key_input, value_input, norm_gain, cotangent):
    sharers = CORES * lax.axis_size("head")
    gain = norm_gain.reshape(1, -1)
    mine, theirs = call(state_kernel, [PIECES, PIECES], key_input, value_input)
    received = swap_cores(theirs)
    (given,) = call(
        send_kernel, [((4, TOK, HALF), F32)], queries, key_input, value_input, cotangent
    )
    got = swap_cores(given)
    (intra,) = call(
        intra_kernel, [BLOCKS], queries, key_input, value_input, got, flops=200_000_000
    )
    chip = scan(mine + received, False)
    raw, low, give, parts = call(
        raw_kernel,
        [BLOCKS, ((HEAD_DIM, HALF), BF16), ((TOK + HEAD_DIM, HALF), F32), ((sharers, 4, TOK), F32)],
        queries, cotangent, gain, got, intra, chip, mine, received,
    )
    parts = over_heads(parts)
    total, here, there = call(
        grad_state_kernel,
        [PIECES, PIECES, PIECES],
        queries, cotangent, gain, got, raw, parts,
    )
    attended, grad_query, grad_kf, grad_vf = call(
        back_kernel,
        [WIDE_LOW, WIDE_LOW, WIDE, WIDE],
        queries, key_input, value_input, cotangent, gain, raw, low, swap_cores(give), parts,
        flops=500_000_000,
    )
    chip = scan(total, True)
    grad_key, grad_value = call(
        last_kernel,
        [WIDE_LOW, WIDE_LOW],
        key_input, value_input, grad_kf, grad_vf, chip, here, swap_cores(chip + there),
    )
    return (attended, grad_query, grad_key, grad_value)


def solution(mesh):
    in_specs = (P("ctx", "head"), P("ctx", "head"), P("ctx", "head"), P("head"), P("ctx", "head"))
    out_specs = (P("ctx", "head"), P("ctx", "head"), P("ctx", "head"), P("ctx", "head"))
    return jax.shard_map(
        per_device, mesh=mesh, in_specs=in_specs, out_specs=out_specs, check_vma=False
    )
```

```python
import jax
import jax.numpy as jnp
from jax import lax
from jax.experimental import pallas as pl
from jax.experimental.pallas import tpu as pltpu
from jax.sharding import PartitionSpec as P

HEAD_DIM = 96
D = 6144
TOK = 128
LANES = 128
HALF_HEADS = 4
HALF = HALF_HEADS * HEAD_DIM
CHIPS = 64
CORES = 2
PIECE = 640

epsilon = 1e-06
F32 = jnp.float32
BF16 = jnp.bfloat16
VMEM = pl.BlockSpec(memory_space=pltpu.VMEM)
NN = (((1,), (0,)), ((), ()))
NT = (((1,), (1,)), ((), ()))
TN = (((0,), (0,)), ((), ()))


def mm(a, b, dims):
    return lax.dot_general(a, b, dims, preferred_element_type=F32)


def half(g):
    return slice(g * HALF, (g + 1) * HALF)


def head_masks(rows):
    lane = lax.broadcasted_iota(jnp.int32, (rows, HALF), 1)
    return [(lane >= h * HEAD_DIM) & (lane < (h + 1) * HEAD_DIM) for h in range(HALF_HEADS)]


def spread(x):
    return jnp.concatenate([x * m.astype(BF16) for m in head_masks(x.shape[0])], axis=0)


def diagonal(x):
    rows = x.shape[0] // HALF_HEADS
    masks = head_masks(rows)
    out = x[:rows]
    for h in range(1, HALF_HEADS):
        out = jnp.where(masks[h], x[h * rows : (h + 1) * rows], out)
    return out


def to_pieces(state):
    rest = state[64:96]
    tail = rest[:, 256:384]
    return jnp.concatenate(
        [
            state[0:64],
            jnp.concatenate([rest[:, 0:128], rest[:, 128:256]], axis=0),
            jnp.concatenate([tail, pltpu.roll(tail, 64, 1)], axis=0),
        ],
        axis=1,
    )


def from_pieces(pieces):
    low = lax.broadcasted_iota(jnp.int32, (32, LANES), 1) < 64
    tail = jnp.where(low, pieces[0:32, 512:640], pltpu.roll(pieces[32:64, 512:640], 64, 1))
    rest = jnp.concatenate([pieces[0:32, 384:512], pieces[32:64, 384:512], tail], axis=1)
    return jnp.concatenate([pieces[:, 0:384], rest], axis=0)


def silu_low(x):
    x = x.astype(F32)
    return (x * jax.nn.sigmoid(x)).astype(BF16)


def silu_slope(x):
    x = x.astype(F32)
    sig = jax.nn.sigmoid(x)
    return sig * (1.0 + x * (1.0 - sig))


def causal4():
    row = lax.broadcasted_iota(jnp.int32, (TOK, TOK), 0)
    col = lax.broadcasted_iota(jnp.int32, (TOK, TOK), 1)
    keep = jnp.where(row >= col, 1.0, 0.0)
    return jnp.concatenate([keep] * HALF_HEADS, axis=1) > 0.5


def by_head(x):
    return jnp.concatenate([x[:, h * TOK : (h + 1) * TOK] for h in range(HALF_HEADS)], axis=0)


def core_index():
    return lax.axis_index("ctx") % CORES


def pick(own, x):
    first = (core_index() == 0) == own
    return jnp.where(first, x[:, half(0)], x[:, half(1)])


def in_order(own, other):
    first = core_index() == 0
    return jnp.where(first, own, other), jnp.where(first, other, own)


def state_kernel(k_hbm, v_hbm, mine_ref, theirs_ref, k_ref, v_ref, sems):
    copies = []
    for g in range(CORES):
        pair = []
        for i, (source, target) in enumerate(((k_hbm, k_ref), (v_hbm, v_ref))):
            copy = pltpu.make_async_copy(
                source.at[:, pl.ds(g * HALF, HALF)], target.at[g], sems.at[2 * g + i]
            )
            copy.start()
            pair.append(copy)
        copies.append(pair)
    states = []
    for g in range(CORES):
        for copy in copies[g]:
            copy.wait()
        states.append(to_pieces(diagonal(mm(silu_low(k_ref[g]), v_ref[g], TN))))
    low = core_index() == 0
    mine_ref[:, 0, :] = jnp.where(low, states[0], states[1])
    theirs_ref[:, 0, :] = jnp.where(low, states[1], states[0])


def send_kernel(after_ref, q_ref, k_ref, v_ref, c_ref, out_ref):
    for i, ref in enumerate((q_ref, k_ref, v_ref, c_ref)):
        out_ref[i] = pick(False, ref[...]).astype(F32)


def attention(q_feat, k_feat):
    return jnp.where(causal4(), mm(q_feat, spread(k_feat), NT), 0.0).astype(BF16)


def intra_kernel(
    q_ref, k_ref, v_ref, c_ref, gain_ref, got_ref, mine_ref, received_ref,
    intra_ref, q_feat_ref, upstream_ref, extra_ref,
):
    core = core_index()
    gain = pick(True, gain_ref[...])
    mine = [pick(True, ref[...]) for ref in (q_ref, k_ref, v_ref, c_ref)]
    others = [got_ref[i].astype(BF16) for i in range(4)]
    for i, (q, k, v, c) in enumerate((mine, others)):
        q_feat = silu_low(q)
        q_feat_ref[i] = q_feat
        upstream_ref[i] = c.astype(F32) * gain
        intra_ref[i] = mm(attention(q_feat, silu_low(k)), spread(v), NN)
    extra_ref[0] = from_pieces(jnp.where(core == 1, received_ref[:, 0, :], 0.0))
    extra_ref[1] = from_pieces(jnp.where(core == 0, mine_ref[:, 0, :], 0.0))


def scan_kernel(backward, pieces_ref, after_ref, out_ref, done_ref):
    row = lax.broadcasted_iota(jnp.int32, (CHIPS, CHIPS), 0)
    col = lax.broadcasted_iota(jnp.int32, (CHIPS, CHIPS), 1)
    before = jnp.where(row < col if backward else row > col, 1.0, 0.0).astype(BF16)
    rest = pieces_ref[:, 0, :]
    terms = []
    for _ in range(3):
        term = rest.astype(BF16)
        rest = rest - term.astype(F32)
        terms.append(term)
    out_ref[:, 0, :] = mm(
        jnp.concatenate([before] * 3, axis=1), jnp.concatenate(terms, axis=0), NN
    )
    done_ref[...] = jnp.zeros_like(done_ref)


def lane_sums(x):
    part = x[:, 0:LANES]
    for i in range(1, x.shape[1] // LANES):
        part = part + x[:, i * LANES : (i + 1) * LANES]
    return jnp.sum(part.T, axis=0, keepdims=True)


def raw_kernel(q_feat_ref, upstream_ref, intra_ref, extra_ref, chip_ref, raw_ref, prefix_ref, parts_ref):
    chip = from_pieces(chip_ref[:, 0, :])
    sums = []
    for i in range(CORES):
        state = (chip + extra_ref[i]).astype(BF16)
        prefix_ref[i] = state
        raw = intra_ref[i] + mm(q_feat_ref[i], spread(state), NN)
        raw_ref[i] = raw
        sums.append(
            jnp.concatenate([lane_sums(raw * raw), lane_sums(upstream_ref[i] * raw)], axis=0)
        )
    sums = jnp.concatenate(in_order(*sums), axis=0)
    parts_ref[...] = jnp.broadcast_to(sums[None], parts_ref.shape)


def scales(totals):
    square = jnp.broadcast_to(totals[0:1], (TOK, LANES)).T
    cross = jnp.broadcast_to(totals[1:2], (TOK, LANES)).T
    mean = square * (1.0 / D) + epsilon
    pair = lax.rsqrt(mean), cross / (D * mean)
    return [jnp.concatenate([x] * (HALF // LANES), axis=1) for x in pair]


def gradient(upstream, raw, inverse, pull):
    return ((upstream - raw * pull) * inverse).astype(BF16)


def own_and_other(parts_ref):
    totals = jnp.sum(parts_ref[...], axis=0)
    return in_order(totals[0:2], totals[2:4])


def grad_state_kernel(
    q_feat_ref, upstream_ref, raw_ref, prefix_ref, parts_ref,
    sum_ref, here_ref, there_ref, give_ref,
):
    core = core_index()
    states = []
    for i, totals in enumerate(own_and_other(parts_ref)):
        d_raw = gradient(upstream_ref[i], raw_ref[i], *scales(totals))
        states.append(diagonal(mm(q_feat_ref[i], d_raw, TN)))
    own, other = states
    sum_ref[:, 0, :] = to_pieces(own + other)
    here_ref[...] = jnp.where(core == 0, other, 0.0)
    there_ref[:, 0, :] = to_pieces(jnp.where(core == 1, own, 0.0))
    give_ref[0:TOK, :] = raw_ref[1]
    give_ref[TOK:, :] = prefix_ref[1].astype(F32)


def back_kernel(
    q_ref, k_ref, v_ref, c_ref, gain_ref, raw_ref, prefix_ref, got_ref, parts_ref,
    attended_ref, grad_q_ref, grad_kf_ref, grad_vf_ref, k_feat_ref, slope_ref, done_ref,
):
    keep = causal4()
    inverse, pull = scales(own_and_other(parts_ref)[0])
    raws = in_order(raw_ref[0], got_ref[0:TOK])
    prefixes = in_order(prefix_ref[0].astype(F32), got_ref[TOK:])
    for g in range(CORES):
        q, k, raw, gain = q_ref[:, half(g)], k_ref[:, half(g)], raws[g], gain_ref[:, half(g)]
        q_feat, k_feat = silu_low(q), silu_low(k)
        k_feat_ref[:, half(g)] = k_feat
        slope_ref[:, half(g)] = silu_slope(k)
        attended_ref[:, half(g)] = (raw * inverse * gain).astype(BF16)
        d_raw = gradient(c_ref[:, half(g)].astype(F32) * gain, raw, inverse, pull)
        back = jnp.where(keep, mm(d_raw, spread(v_ref[:, half(g)]), NT), 0.0).astype(BF16)
        grad_qf = mm(back, spread(k_feat), NN) + mm(d_raw, spread(prefixes[g].astype(BF16)), NT)
        grad_q_ref[:, half(g)] = (grad_qf * silu_slope(q)).astype(BF16)
        grad_kf_ref[:, half(g)] = mm(by_head(back), spread(q_feat), TN)
        grad_vf_ref[:, half(g)] = mm(by_head(attention(q_feat, k_feat)), spread(d_raw), TN)
    done_ref[...] = jnp.zeros_like(done_ref)


def finished(own, refs, later):
    v, k_feat, slope, grad_kf, grad_vf = (pick(own, ref[...]) for ref in refs)
    later = spread(later.astype(BF16))
    grad_k = (grad_kf + mm(v, later, NT)) * slope
    return grad_k.astype(BF16), (grad_vf + mm(k_feat, later, NN)).astype(BF16)


def own_kernel(
    v_ref, k_feat_ref, slope_ref, grad_kf_ref, grad_vf_ref, chip_ref, here_ref, grad_k_ref, grad_v_ref
):
    refs = v_ref, k_feat_ref, slope_ref, grad_kf_ref, grad_vf_ref
    later = from_pieces(chip_ref[:, 0, :]) + here_ref[...]
    grad_k_ref[...], grad_v_ref[...] = finished(True, refs, later)


def last_kernel(
    v_ref, k_feat_ref, slope_ref, grad_kf_ref, grad_vf_ref, there_ref, own_k_ref, own_v_ref,
    grad_k_hbm, grad_v_hbm, k_ref, other_ref, sems,
):
    core = core_index()
    own = pl.ds(pl.multiple_of(core * HALF, HALF), HALF)
    other = pl.ds(pl.multiple_of((1 - core) * HALF, HALF), HALF)
    copies = [
        pltpu.make_async_copy(own_k_ref, grad_k_hbm.at[:, own], sems.at[0]),
        pltpu.make_async_copy(own_v_ref, grad_v_hbm.at[:, own], sems.at[1]),
        pltpu.make_async_copy(k_ref, grad_k_hbm.at[:, other], sems.at[2]),
        pltpu.make_async_copy(other_ref, grad_v_hbm.at[:, other], sems.at[3]),
    ]
    copies[0].start()
    copies[1].start()
    refs = v_ref, k_feat_ref, slope_ref, grad_kf_ref, grad_vf_ref
    k_ref[...], other_ref[...] = finished(False, refs, from_pieces(there_ref[:, 0, :]))
    copies[2].start()
    copies[3].start()
    for copy in copies:
        copy.wait()


def call(kernel, outs, *args, flops=0, in_hbm=False, out_hbm=False, scratch=(), room=32):
    in_space, out_space = (
        pl.BlockSpec(memory_space=pltpu.HBM) if far else VMEM for far in (in_hbm, out_hbm)
    )
    return pl.pallas_call(
        kernel,
        out_shape=[jax.ShapeDtypeStruct(shape, kind) for shape, kind in outs],
        in_specs=[in_space] * len(args),
        out_specs=[out_space] * len(outs),
        scratch_shapes=list(scratch),
        compiler_params=pltpu.CompilerParams(vmem_limit_bytes=room * 1024 * 1024),
        cost_estimate=pl.CostEstimate(flops=flops, bytes_accessed=1_000_000, transcendentals=0),
    )(*args)


def swap_cores(x):
    pairs = [(i, i ^ 1) for i in range(CHIPS * CORES)]
    return lax.ppermute(x, "ctx", pairs)


def across_chips(x):
    groups = [[chip * CORES + core for chip in range(CHIPS)] for core in range(CORES)]
    return lax.all_to_all(x, "ctx", 0, 0, axis_index_groups=groups)


def over_heads(x):
    size = CORES * lax.axis_size("head")
    groups = [[chip * size + i for i in range(size)] for chip in range(CHIPS)]
    return lax.all_to_all(x, ("ctx", "head"), 0, 0, axis_index_groups=groups)


PIECES = ((CHIPS, 1, PIECE), F32)
DONE = ((8, LANES), F32)
WIDE = ((TOK, CORES * HALF), F32)
WIDE_LOW = ((TOK, CORES * HALF), BF16)
HALF_LOW = ((TOK, HALF), BF16)
BLOCKS = ((CORES, TOK, HALF), F32)
BLOCKS_LOW = ((CORES, TOK, HALF), BF16)


def scan_sums(pieces, after, backward):
    def kernel(*refs):
        scan_kernel(backward, *refs)

    return call(kernel, [PIECES, DONE], pieces, after)


def per_device(queries, key_input, value_input, norm_gain, cotangent):
    sharers = CORES * lax.axis_size("head")
    gain = norm_gain.reshape(1, -1)
    load = [pltpu.VMEM((CORES, TOK, HALF), BF16)] * 2 + [pltpu.SemaphoreType.DMA((4,))]
    mine, theirs = call(
        state_kernel, [PIECES, PIECES], key_input, value_input, in_hbm=True, scratch=load, room=60
    )
    received = swap_cores(theirs)
    summed, done = scan_sums(across_chips(mine + received), jnp.zeros(*DONE), False)
    (given,) = call(
        send_kernel, [((4, TOK, HALF), F32)], done, queries, key_input, value_input, cotangent
    )
    got = swap_cores(given)
    intra, q_feat, upstream, extra = call(
        intra_kernel,
        [BLOCKS, BLOCKS_LOW, BLOCKS, ((CORES, HEAD_DIM, HALF), F32)],
        queries, key_input, value_input, cotangent, gain, got, mine, received,
        flops=200_000_000,
    )
    raw, prefix, parts = call(
        raw_kernel,
        [BLOCKS, ((CORES, HEAD_DIM, HALF), BF16), ((sharers, 4, TOK), F32)],
        q_feat, upstream, intra, extra, across_chips(summed),
    )
    parts = over_heads(parts)
    total, here, there, give = call(
        grad_state_kernel,
        [PIECES, ((HEAD_DIM, HALF), F32), PIECES, ((TOK + HEAD_DIM, HALF), F32)],
        q_feat, upstream, raw, prefix, parts,
    )
    attended, grad_query, grad_kf, grad_vf, k_feat, slope, done = call(
        back_kernel,
        [WIDE_LOW, WIDE_LOW, WIDE, WIDE, WIDE_LOW, WIDE, DONE],
        queries, key_input, value_input, cotangent, gain, raw, prefix, swap_cores(give), parts,
        flops=500_000_000,
    )
    summed, _ = scan_sums(across_chips(total), done, True)
    chip = across_chips(summed)
    there = swap_cores(chip + there)
    parts = value_input, k_feat, slope, grad_kf, grad_vf
    own = call(own_kernel, [HALF_LOW, HALF_LOW], *parts, chip, here, flops=50_000_000)
    store = [pltpu.VMEM((TOK, HALF), BF16)] * 2 + [pltpu.SemaphoreType.DMA((4,))]
    grad_key, grad_value = call(
        last_kernel, [WIDE_LOW, WIDE_LOW], *parts, there, *own, out_hbm=True, scratch=store
    )
    return (attended, grad_query, grad_key, grad_value)


def solution(mesh):
    in_specs = (P("ctx", "head"), P("ctx", "head"), P("ctx", "head"), P("head"), P("ctx", "head"))
    out_specs = (P("ctx", "head"), P("ctx", "head"), P("ctx", "head"), P("ctx", "head"))
    return jax.shard_map(
        per_device, mesh=mesh, in_specs=in_specs, out_specs=out_specs, check_vma=False
    )
```

```python
import jax
import jax.numpy as jnp
from jax import lax
from jax.experimental import pallas as pl
from jax.experimental.pallas import tpu as pltpu
from jax.sharding import PartitionSpec as P

HEAD_DIM = 96
D = 6144
TOK = 128
LANES = 128
HALF_HEADS = 4
HALF = HALF_HEADS * HEAD_DIM
CHIPS = 64
CORES = 2
PIECE = 640

epsilon = 1e-06
F32 = jnp.float32
BF16 = jnp.bfloat16
VMEM = pl.BlockSpec(memory_space=pltpu.VMEM)
NN = (((1,), (0,)), ((), ()))
NT = (((1,), (1,)), ((), ()))
TN = (((0,), (0,)), ((), ()))


def mm(a, b, dims):
    return lax.dot_general(a, b, dims, preferred_element_type=F32)


def half(g):
    return slice(g * HALF, (g + 1) * HALF)


def head_masks(rows):
    lane = lax.broadcasted_iota(jnp.int32, (rows, HALF), 1)
    return [(lane >= h * HEAD_DIM) & (lane < (h + 1) * HEAD_DIM) for h in range(HALF_HEADS)]


def spread(x):
    return jnp.concatenate([x * m.astype(BF16) for m in head_masks(x.shape[0])], axis=0)


def diagonal(x):
    rows = x.shape[0] // HALF_HEADS
    masks = head_masks(rows)
    out = x[:rows]
    for h in range(1, HALF_HEADS):
        out = jnp.where(masks[h], x[h * rows : (h + 1) * rows], out)
    return out


def to_pieces(state):
    rest = state[64:96]
    tail = rest[:, 256:384]
    return jnp.concatenate(
        [
            state[0:64],
            jnp.concatenate([rest[:, 0:128], rest[:, 128:256]], axis=0),
            jnp.concatenate([tail, pltpu.roll(tail, 64, 1)], axis=0),
        ],
        axis=1,
    )


def from_pieces(pieces):
    low = lax.broadcasted_iota(jnp.int32, (32, LANES), 1) < 64
    tail = jnp.where(low, pieces[0:32, 512:640], pltpu.roll(pieces[32:64, 512:640], 64, 1))
    rest = jnp.concatenate([pieces[0:32, 384:512], pieces[32:64, 384:512], tail], axis=1)
    return jnp.concatenate([pieces[:, 0:384], rest], axis=0)


def silu_low(x):
    x = x.astype(F32)
    return (x * jax.nn.sigmoid(x)).astype(BF16)


def silu_slope(x):
    x = x.astype(F32)
    sig = jax.nn.sigmoid(x)
    return sig * (1.0 + x * (1.0 - sig))


def causal4():
    row = lax.broadcasted_iota(jnp.int32, (TOK, TOK), 0)
    col = lax.broadcasted_iota(jnp.int32, (TOK, TOK), 1)
    keep = jnp.where(row >= col, 1.0, 0.0)
    return jnp.concatenate([keep] * HALF_HEADS, axis=1) > 0.5


def by_head(x):
    return jnp.concatenate([x[:, h * TOK : (h + 1) * TOK] for h in range(HALF_HEADS)], axis=0)


def core_index():
    return lax.axis_index("ctx") % CORES


def pick(own, x):
    first = (core_index() == 0) == own
    return jnp.where(first, x[:, half(0)], x[:, half(1)])


def in_order(own, other):
    first = core_index() == 0
    return jnp.where(first, own, other), jnp.where(first, other, own)


def state_kernel(pair_ref, mine_ref, theirs_ref):
    first, second = (
        to_pieces(diagonal(mm(silu_low(pair_ref[0, :, half(g)]), pair_ref[1, :, half(g)], TN)))
        for g in range(CORES)
    )
    low = core_index() == 0
    mine_ref[:, 0, :] = jnp.where(low, first, second)
    theirs_ref[:, 0, :] = jnp.where(low, second, first)


def send_kernel(q_ref, k_ref, v_ref, c_ref, out_ref):
    for i, ref in enumerate((q_ref, k_ref, v_ref, c_ref)):
        out_ref[i] = pick(False, ref[...]).astype(F32)


def attention(q_feat, k_feat):
    return jnp.where(causal4(), mm(q_feat, spread(k_feat), NT), 0.0).astype(BF16)


def intra_kernel(q_ref, k_ref, v_ref, got_ref, intra_ref):
    mine = [pick(True, ref[...]) for ref in (q_ref, k_ref, v_ref)]
    others = [got_ref[i].astype(BF16) for i in range(3)]
    for i, (q, k, v) in enumerate((mine, others)):
        intra_ref[i] = mm(attention(silu_low(q), silu_low(k)), spread(v), NN)


def scan_kernel(backward, pieces_ref, out_ref):
    row = lax.broadcasted_iota(jnp.int32, (CHIPS, CHIPS), 0)
    col = lax.broadcasted_iota(jnp.int32, (CHIPS, CHIPS), 1)
    before = jnp.where(row < col if backward else row > col, 1.0, 0.0).astype(BF16)
    rest = pieces_ref[:, 0, :]
    terms = []
    for _ in range(3):
        term = rest.astype(BF16)
        rest = rest - term.astype(F32)
        terms.append(term)
    out_ref[:, 0, :] = mm(
        jnp.concatenate([before] * 3, axis=1), jnp.concatenate(terms, axis=0), NN
    )


def lane_sums(x):
    part = x[:, 0:LANES]
    for i in range(1, x.shape[1] // LANES):
        part = part + x[:, i * LANES : (i + 1) * LANES]
    return jnp.sum(part.T, axis=0, keepdims=True)


def raw_kernel(
    q_ref, c_ref, gain_ref, got_ref, intra_ref, chip_ref, mine_ref, received_ref,
    raw_ref, low_ref, give_ref, parts_ref,
):
    core = core_index()
    chip = chip_ref[:, 0, :]
    own = from_pieces(chip + jnp.where(core == 1, received_ref[:, 0, :], 0.0))
    other = from_pieces(chip + jnp.where(core == 0, mine_ref[:, 0, :], 0.0))
    low_ref[...] = own.astype(BF16)
    give_ref[TOK:, :] = other
    gain = pick(True, gain_ref[...])
    q, c = pick(True, q_ref[...]), pick(True, c_ref[...])
    sums = []
    for i, (q, c, state) in enumerate(
        ((q, c, own), (got_ref[0].astype(BF16), got_ref[3], other))
    ):
        raw = intra_ref[i] + mm(silu_low(q), spread(state.astype(BF16)), NN)
        raw_ref[i] = raw
        upstream = c.astype(F32) * gain
        sums.append(jnp.concatenate([lane_sums(raw * raw), lane_sums(upstream * raw)], axis=0))
    give_ref[0:TOK, :] = raw_ref[1]
    sums = jnp.concatenate(in_order(*sums), axis=0)
    parts_ref[...] = jnp.broadcast_to(sums[None], parts_ref.shape)


def scales(totals):
    square = jnp.broadcast_to(totals[0:1], (TOK, LANES)).T
    cross = jnp.broadcast_to(totals[1:2], (TOK, LANES)).T
    mean = square * (1.0 / D) + epsilon
    pair = lax.rsqrt(mean), cross / (D * mean)
    return [jnp.concatenate([x] * (HALF // LANES), axis=1) for x in pair]


def gradient(c, gain, raw, inverse, pull):
    return ((c.astype(F32) * gain - raw * pull) * inverse).astype(BF16)


def own_and_other(parts_ref):
    totals = jnp.sum(parts_ref[...], axis=0)
    return in_order(totals[0:2], totals[2:4])


def grad_state_kernel(
    q_ref, c_ref, gain_ref, got_ref, raw_ref, parts_ref, sum_ref, own_ref, other_ref
):
    gain = pick(True, gain_ref[...])
    q, c = pick(True, q_ref[...]), pick(True, c_ref[...])
    states = []
    for i, (q, c, totals) in enumerate(
        zip((q, got_ref[0].astype(BF16)), (c, got_ref[3]), own_and_other(parts_ref))
    ):
        d_raw = gradient(c, gain, raw_ref[i], *scales(totals))
        states.append(diagonal(mm(silu_low(q), d_raw, TN)))
    own_ref[...], other_ref[...] = states
    sum_ref[:, 0, :] = to_pieces(states[0] + states[1])


def back_kernel(
    q_ref, k_ref, v_ref, c_ref, gain_ref, raw_ref, low_ref, got_ref, parts_ref, own_ref, other_ref,
    attended_ref, grad_q_ref, grad_kf_ref, grad_vf_ref, here_ref, there_ref,
):
    core = core_index()
    here_ref[...] = jnp.where(core == 0, other_ref[...], 0.0)
    there_ref[:, 0, :] = to_pieces(jnp.where(core == 1, own_ref[...], 0.0))
    keep = causal4()
    inverse, pull = scales(own_and_other(parts_ref)[0])
    raws = in_order(raw_ref[0], got_ref[0:TOK])
    lows = in_order(low_ref[...].astype(F32), got_ref[TOK:])
    for g in range(CORES):
        q, raw, gain = q_ref[:, half(g)], raws[g], gain_ref[:, half(g)]
        q_feat, k_feat = silu_low(q), silu_low(k_ref[:, half(g)])
        attended_ref[:, half(g)] = (raw * inverse * gain).astype(BF16)
        d_raw = gradient(c_ref[:, half(g)], gain, raw, inverse, pull)
        back = jnp.where(keep, mm(d_raw, spread(v_ref[:, half(g)]), NT), 0.0).astype(BF16)
        grad_qf = mm(back, spread(k_feat), NN) + mm(d_raw, spread(lows[g].astype(BF16)), NT)
        grad_q_ref[:, half(g)] = (grad_qf * silu_slope(q)).astype(BF16)
        grad_kf_ref[:, half(g)] = mm(by_head(back), spread(q_feat), TN)
        grad_vf_ref[:, half(g)] = mm(by_head(attention(q_feat, k_feat)), spread(d_raw), TN)


def finished(own, refs, later):
    k, v, grad_kf, grad_vf = (pick(own, ref[...]) for ref in refs)
    later = spread(later.astype(BF16))
    grad_k = (grad_kf + mm(v, later, NT)) * silu_slope(k)
    return grad_k.astype(BF16), (grad_vf + mm(silu_low(k), later, NN)).astype(BF16)


def own_kernel(
    k_ref, v_ref, grad_kf_ref, grad_vf_ref, chip_ref, here_ref, grad_k_ref, grad_v_ref
):
    later = from_pieces(chip_ref[:, 0, :]) + here_ref[...]
    refs = k_ref, v_ref, grad_kf_ref, grad_vf_ref
    grad_k_ref[...], grad_v_ref[...] = finished(True, refs, later)


def last_kernel(
    k_ref, v_ref, grad_kf_ref, grad_vf_ref, there_ref, own_k_ref, own_v_ref,
    grad_k_hbm, grad_v_hbm, other_k_ref, other_v_ref, sems,
):
    core = core_index()
    own = pl.ds(pl.multiple_of(core * HALF, HALF), HALF)
    other = pl.ds(pl.multiple_of((1 - core) * HALF, HALF), HALF)
    copies = [
        pltpu.make_async_copy(own_k_ref, grad_k_hbm.at[:, own], sems.at[0]),
        pltpu.make_async_copy(own_v_ref, grad_v_hbm.at[:, own], sems.at[1]),
        pltpu.make_async_copy(other_k_ref, grad_k_hbm.at[:, other], sems.at[2]),
        pltpu.make_async_copy(other_v_ref, grad_v_hbm.at[:, other], sems.at[3]),
    ]
    copies[0].start()
    copies[1].start()
    refs = k_ref, v_ref, grad_kf_ref, grad_vf_ref
    later = from_pieces(there_ref[:, 0, :])
    other_k_ref[...], other_v_ref[...] = finished(False, refs, later)
    copies[2].start()
    copies[3].start()
    for copy in copies:
        copy.wait()


def call(kernel, outs, *args, flops=0, out_space=VMEM, scratch=()):
    return pl.pallas_call(
        kernel,
        out_shape=[jax.ShapeDtypeStruct(shape, kind) for shape, kind in outs],
        in_specs=[VMEM] * len(args),
        out_specs=[out_space] * len(outs),
        scratch_shapes=list(scratch),
        compiler_params=pltpu.CompilerParams(vmem_limit_bytes=32 * 1024 * 1024),
        cost_estimate=pl.CostEstimate(flops=flops, bytes_accessed=1_000_000, transcendentals=0),
    )(*args)


def swap_cores(x):
    pairs = [(i, i ^ 1) for i in range(CHIPS * CORES)]
    return lax.ppermute(x, "ctx", pairs)


def across_chips(x):
    groups = [[chip * CORES + core for chip in range(CHIPS)] for core in range(CORES)]
    return lax.all_to_all(x, "ctx", 0, 0, axis_index_groups=groups)


def over_heads(x):
    size = CORES * lax.axis_size("head")
    groups = [[chip * size + i for i in range(size)] for chip in range(CHIPS)]
    return lax.all_to_all(x, ("ctx", "head"), 0, 0, axis_index_groups=groups)


PIECES = ((CHIPS, 1, PIECE), F32)
WIDE = ((TOK, CORES * HALF), F32)
WIDE_LOW = ((TOK, CORES * HALF), BF16)
STATE = ((HEAD_DIM, HALF), F32)
HALF_LOW = ((TOK, HALF), BF16)
BLOCKS = ((CORES, TOK, HALF), F32)


def scan(pieces, backward):
    def kernel(pieces_ref, out_ref):
        scan_kernel(backward, pieces_ref, out_ref)

    (summed,) = call(kernel, [PIECES], across_chips(pieces))
    return across_chips(summed)


def per_device(queries, key_input, value_input, norm_gain, cotangent):
    sharers = CORES * lax.axis_size("head")
    gain = norm_gain.reshape(1, -1)
    mine, theirs = call(state_kernel, [PIECES, PIECES], jnp.stack([key_input, value_input]))
    received = swap_cores(theirs)
    (given,) = call(
        send_kernel, [((4, TOK, HALF), F32)], queries, key_input, value_input, cotangent
    )
    got = swap_cores(given)
    (intra,) = call(
        intra_kernel, [BLOCKS], queries, key_input, value_input, got, flops=200_000_000
    )
    chip = scan(mine + received, False)
    raw, low, give, parts = call(
        raw_kernel,
        [BLOCKS, ((HEAD_DIM, HALF), BF16), ((TOK + HEAD_DIM, HALF), F32), ((sharers, 4, TOK), F32)],
        queries, cotangent, gain, got, intra, chip, mine, received,
    )
    parts = over_heads(parts)
    total, own, other = call(
        grad_state_kernel,
        [PIECES, STATE, STATE],
        queries, cotangent, gain, got, raw, parts,
    )
    attended, grad_query, grad_kf, grad_vf, here, there = call(
        back_kernel,
        [WIDE_LOW, WIDE_LOW, WIDE, WIDE, STATE, PIECES],
        queries, key_input, value_input, cotangent, gain, raw, low, swap_cores(give), parts,
        own, other,
        flops=500_000_000,
    )
    chip = scan(total, True)
    there = swap_cores(chip + there)
    parts = key_input, value_input, grad_kf, grad_vf
    own = call(own_kernel, [HALF_LOW, HALF_LOW], *parts, chip, here, flops=50_000_000)
    store = [pltpu.VMEM(*HALF_LOW)] * 2 + [pltpu.SemaphoreType.DMA((4,))]
    grad_key, grad_value = call(
        last_kernel,
        [WIDE_LOW, WIDE_LOW],
        *parts, there, *own,
        out_space=pl.BlockSpec(memory_space=pltpu.HBM),
        scratch=store,
    )
    return (attended, grad_query, grad_key, grad_value)


def solution(mesh):
    in_specs = (P("ctx", "head"), P("ctx", "head"), P("ctx", "head"), P("head"), P("ctx", "head"))
    out_specs = (P("ctx", "head"), P("ctx", "head"), P("ctx", "head"), P("ctx", "head"))
    return jax.shard_map(
        per_device, mesh=mesh, in_specs=in_specs, out_specs=out_specs, check_vma=False
    )
```

```python
import jax
import jax.numpy as jnp
from jax import lax
from jax.experimental import pallas as pl
from jax.experimental.pallas import tpu as pltpu
from jax.sharding import PartitionSpec as P

HEAD_DIM = 96
D = 6144
TOK = 128
LANES = 128
HALF_HEADS = 4
HALF = HALF_HEADS * HEAD_DIM
CHIPS = 64
CORES = 2
PIECE = 640

epsilon = 1e-06
F32 = jnp.float32
BF16 = jnp.bfloat16
VMEM = pl.BlockSpec(memory_space=pltpu.VMEM)
NN = (((1,), (0,)), ((), ()))
NT = (((1,), (1,)), ((), ()))
TN = (((0,), (0,)), ((), ()))


def mm(a, b, dims):
    return lax.dot_general(a, b, dims, preferred_element_type=F32)


def half(g):
    return slice(g * HALF, (g + 1) * HALF)


def head_masks(rows):
    lane = lax.broadcasted_iota(jnp.int32, (rows, HALF), 1)
    return [(lane >= h * HEAD_DIM) & (lane < (h + 1) * HEAD_DIM) for h in range(HALF_HEADS)]


def spread(x):
    return jnp.concatenate([x * m.astype(BF16) for m in head_masks(x.shape[0])], axis=0)


def diagonal(x):
    rows = x.shape[0] // HALF_HEADS
    masks = head_masks(rows)
    out = x[:rows]
    for h in range(1, HALF_HEADS):
        out = jnp.where(masks[h], x[h * rows : (h + 1) * rows], out)
    return out


def to_pieces(state):
    rest = state[64:96]
    tail = rest[:, 256:384]
    return jnp.concatenate(
        [
            state[0:64],
            jnp.concatenate([rest[:, 0:128], rest[:, 128:256]], axis=0),
            jnp.concatenate([tail, pltpu.roll(tail, 64, 1)], axis=0),
        ],
        axis=1,
    )


def from_pieces(pieces):
    low = lax.broadcasted_iota(jnp.int32, (32, LANES), 1) < 64
    tail = jnp.where(low, pieces[0:32, 512:640], pltpu.roll(pieces[32:64, 512:640], 64, 1))
    rest = jnp.concatenate([pieces[0:32, 384:512], pieces[32:64, 384:512], tail], axis=1)
    return jnp.concatenate([pieces[:, 0:384], rest], axis=0)


def silu_low(x):
    x = x.astype(F32)
    return (x * jax.nn.sigmoid(x)).astype(BF16)


def silu_slope(x):
    x = x.astype(F32)
    sig = jax.nn.sigmoid(x)
    return sig * (1.0 + x * (1.0 - sig))


def causal4():
    row = lax.broadcasted_iota(jnp.int32, (TOK, TOK), 0)
    col = lax.broadcasted_iota(jnp.int32, (TOK, TOK), 1)
    keep = jnp.where(row >= col, 1.0, 0.0)
    return jnp.concatenate([keep] * HALF_HEADS, axis=1) > 0.5


def by_head(x):
    return jnp.concatenate([x[:, h * TOK : (h + 1) * TOK] for h in range(HALF_HEADS)], axis=0)


def core_index():
    return lax.axis_index("ctx") % CORES


def pick(own, x):
    first = (core_index() == 0) == own
    return jnp.where(first, x[:, half(0)], x[:, half(1)])


def in_order(own, other):
    first = core_index() == 0
    return jnp.where(first, own, other), jnp.where(first, other, own)


def state_kernel(pair_ref, mine_ref, theirs_ref):
    first, second = (
        to_pieces(diagonal(mm(silu_low(pair_ref[0, :, half(g)]), pair_ref[1, :, half(g)], TN)))
        for g in range(CORES)
    )
    low = core_index() == 0
    mine_ref[:, 0, :] = jnp.where(low, first, second)
    theirs_ref[:, 0, :] = jnp.where(low, second, first)


def send_kernel(q_ref, k_ref, v_ref, c_ref, out_ref):
    for i, ref in enumerate((q_ref, k_ref, v_ref, c_ref)):
        out_ref[i] = pick(False, ref[...]).astype(F32)


def attention(q_feat, k_feat):
    return jnp.where(causal4(), mm(q_feat, spread(k_feat), NT), 0.0).astype(BF16)


def intra_kernel(q_ref, k_ref, v_ref, got_ref, intra_ref):
    mine = [pick(True, ref[...]) for ref in (q_ref, k_ref, v_ref)]
    others = [got_ref[i].astype(BF16) for i in range(3)]
    for i, (q, k, v) in enumerate((mine, others)):
        intra_ref[i] = mm(attention(silu_low(q), silu_low(k)), spread(v), NN)


def scan_kernel(backward, pieces_ref, out_ref):
    total = jnp.zeros((1, PIECE), F32)
    for i in range(CHIPS):
        chip = CHIPS - 1 - i if backward else i
        out_ref[chip] = total
        total = total + pieces_ref[chip]


def lane_sums(x):
    part = x[:, 0:LANES]
    for i in range(1, x.shape[1] // LANES):
        part = part + x[:, i * LANES : (i + 1) * LANES]
    return jnp.sum(part.T, axis=0, keepdims=True)


def raw_kernel(
    q_ref, c_ref, gain_ref, got_ref, intra_ref, chip_ref, mine_ref, received_ref,
    raw_ref, low_ref, give_ref, parts_ref,
):
    core = core_index()
    chip = chip_ref[:, 0, :]
    own = from_pieces(chip + jnp.where(core == 1, received_ref[:, 0, :], 0.0))
    other = from_pieces(chip + jnp.where(core == 0, mine_ref[:, 0, :], 0.0))
    low_ref[...] = own.astype(BF16)
    give_ref[TOK:, :] = other
    gain = pick(True, gain_ref[...])
    q, c = pick(True, q_ref[...]), pick(True, c_ref[...])
    sums = []
    for i, (q, c, state) in enumerate(
        ((q, c, own), (got_ref[0].astype(BF16), got_ref[3], other))
    ):
        raw = intra_ref[i] + mm(silu_low(q), spread(state.astype(BF16)), NN)
        raw_ref[i] = raw
        upstream = c.astype(F32) * gain
        sums.append(jnp.concatenate([lane_sums(raw * raw), lane_sums(upstream * raw)], axis=0))
    give_ref[0:TOK, :] = raw_ref[1]
    sums = jnp.concatenate(in_order(*sums), axis=0)
    parts_ref[...] = jnp.broadcast_to(sums[None], parts_ref.shape)


def scales(totals):
    square = jnp.broadcast_to(totals[0:1], (TOK, LANES)).T
    cross = jnp.broadcast_to(totals[1:2], (TOK, LANES)).T
    mean = square * (1.0 / D) + epsilon
    pair = lax.rsqrt(mean), cross / (D * mean)
    return [jnp.concatenate([x] * (HALF // LANES), axis=1) for x in pair]


def gradient(c, gain, raw, inverse, pull):
    return ((c.astype(F32) * gain - raw * pull) * inverse).astype(BF16)


def own_and_other(parts_ref):
    totals = jnp.sum(parts_ref[...], axis=0)
    return in_order(totals[0:2], totals[2:4])


def grad_state_kernel(
    q_ref, c_ref, gain_ref, got_ref, raw_ref, parts_ref, sum_ref, own_ref, other_ref
):
    gain = pick(True, gain_ref[...])
    q, c = pick(True, q_ref[...]), pick(True, c_ref[...])
    states = []
    for i, (q, c, totals) in enumerate(
        zip((q, got_ref[0].astype(BF16)), (c, got_ref[3]), own_and_other(parts_ref))
    ):
        d_raw = gradient(c, gain, raw_ref[i], *scales(totals))
        states.append(diagonal(mm(silu_low(q), d_raw, TN)))
    own_ref[...], other_ref[...] = states
    sum_ref[:, 0, :] = to_pieces(states[0] + states[1])


def back_kernel(
    q_ref, k_ref, v_ref, c_ref, gain_ref, raw_ref, low_ref, got_ref, parts_ref, own_ref, other_ref,
    attended_ref, grad_q_ref, grad_kf_ref, grad_vf_ref, here_ref, there_ref,
):
    core = core_index()
    here_ref[...] = jnp.where(core == 0, other_ref[...], 0.0)
    there_ref[:, 0, :] = to_pieces(jnp.where(core == 1, own_ref[...], 0.0))
    keep = causal4()
    inverse, pull = scales(own_and_other(parts_ref)[0])
    raws = in_order(raw_ref[0], got_ref[0:TOK])
    lows = in_order(low_ref[...].astype(F32), got_ref[TOK:])
    for g in range(CORES):
        q, raw, gain = q_ref[:, half(g)], raws[g], gain_ref[:, half(g)]
        q_feat, k_feat = silu_low(q), silu_low(k_ref[:, half(g)])
        attended_ref[:, half(g)] = (raw * inverse * gain).astype(BF16)
        d_raw = gradient(c_ref[:, half(g)], gain, raw, inverse, pull)
        back = jnp.where(keep, mm(d_raw, spread(v_ref[:, half(g)]), NT), 0.0).astype(BF16)
        grad_qf = mm(back, spread(k_feat), NN) + mm(d_raw, spread(lows[g].astype(BF16)), NT)
        grad_q_ref[:, half(g)] = (grad_qf * silu_slope(q)).astype(BF16)
        grad_kf_ref[:, half(g)] = mm(by_head(back), spread(q_feat), TN)
        grad_vf_ref[:, half(g)] = mm(by_head(attention(q_feat, k_feat)), spread(d_raw), TN)


def finished(own, refs, later):
    k, v, grad_kf, grad_vf = (pick(own, ref[...]) for ref in refs)
    later = spread(later.astype(BF16))
    grad_k = (grad_kf + mm(v, later, NT)) * silu_slope(k)
    return grad_k.astype(BF16), (grad_vf + mm(silu_low(k), later, NN)).astype(BF16)


def own_kernel(
    k_ref, v_ref, grad_kf_ref, grad_vf_ref, chip_ref, here_ref, grad_k_ref, grad_v_ref
):
    later = from_pieces(chip_ref[:, 0, :]) + here_ref[...]
    refs = k_ref, v_ref, grad_kf_ref, grad_vf_ref
    grad_k_ref[...], grad_v_ref[...] = finished(True, refs, later)


def last_kernel(
    k_ref, v_ref, grad_kf_ref, grad_vf_ref, there_ref, own_k_ref, own_v_ref,
    grad_k_hbm, grad_v_hbm, other_k_ref, other_v_ref, sems,
):
    core = core_index()
    own = pl.ds(pl.multiple_of(core * HALF, HALF), HALF)
    other = pl.ds(pl.multiple_of((1 - core) * HALF, HALF), HALF)
    copies = [
        pltpu.make_async_copy(own_k_ref, grad_k_hbm.at[:, own], sems.at[0]),
        pltpu.make_async_copy(own_v_ref, grad_v_hbm.at[:, own], sems.at[1]),
        pltpu.make_async_copy(other_k_ref, grad_k_hbm.at[:, other], sems.at[2]),
        pltpu.make_async_copy(other_v_ref, grad_v_hbm.at[:, other], sems.at[3]),
    ]
    copies[0].start()
    copies[1].start()
    refs = k_ref, v_ref, grad_kf_ref, grad_vf_ref
    later = from_pieces(there_ref[:, 0, :])
    other_k_ref[...], other_v_ref[...] = finished(False, refs, later)
    copies[2].start()
    copies[3].start()
    for copy in copies:
        copy.wait()


def call(kernel, outs, *args, flops=0, out_space=VMEM, scratch=()):
    return pl.pallas_call(
        kernel,
        out_shape=[jax.ShapeDtypeStruct(shape, kind) for shape, kind in outs],
        in_specs=[VMEM] * len(args),
        out_specs=[out_space] * len(outs),
        scratch_shapes=list(scratch),
        compiler_params=pltpu.CompilerParams(vmem_limit_bytes=32 * 1024 * 1024),
        cost_estimate=pl.CostEstimate(flops=flops, bytes_accessed=1_000_000, transcendentals=0),
    )(*args)


def swap_cores(x):
    pairs = [(i, i ^ 1) for i in range(CHIPS * CORES)]
    return lax.ppermute(x, "ctx", pairs)


def across_chips(x):
    groups = [[chip * CORES + core for chip in range(CHIPS)] for core in range(CORES)]
    return lax.all_to_all(x, "ctx", 0, 0, axis_index_groups=groups)


def over_heads(x):
    size = CORES * lax.axis_size("head")
    groups = [[chip * size + i for i in range(size)] for chip in range(CHIPS)]
    return lax.all_to_all(x, ("ctx", "head"), 0, 0, axis_index_groups=groups)


PIECES = ((CHIPS, 1, PIECE), F32)
WIDE = ((TOK, CORES * HALF), F32)
WIDE_LOW = ((TOK, CORES * HALF), BF16)
STATE = ((HEAD_DIM, HALF), F32)
HALF_LOW = ((TOK, HALF), BF16)
BLOCKS = ((CORES, TOK, HALF), F32)


def scan(pieces, backward):
    def kernel(pieces_ref, out_ref):
        scan_kernel(backward, pieces_ref, out_ref)

    (summed,) = call(kernel, [PIECES], across_chips(pieces))
    return across_chips(summed)


def per_device(queries, key_input, value_input, norm_gain, cotangent):
    sharers = CORES * lax.axis_size("head")
    gain = norm_gain.reshape(1, -1)
    mine, theirs = call(state_kernel, [PIECES, PIECES], jnp.stack([key_input, value_input]))
    received = swap_cores(theirs)
    (given,) = call(
        send_kernel, [((4, TOK, HALF), F32)], queries, key_input, value_input, cotangent
    )
    got = swap_cores(given)
    (intra,) = call(
        intra_kernel, [BLOCKS], queries, key_input, value_input, got, flops=200_000_000
    )
    chip = scan(mine + received, False)
    raw, low, give, parts = call(
        raw_kernel,
        [BLOCKS, ((HEAD_DIM, HALF), BF16), ((TOK + HEAD_DIM, HALF), F32), ((sharers, 4, TOK), F32)],
        queries, cotangent, gain, got, intra, chip, mine, received,
    )
    parts = over_heads(parts)
    total, own, other = call(
        grad_state_kernel,
        [PIECES, STATE, STATE],
        queries, cotangent, gain, got, raw, parts,
    )
    attended, grad_query, grad_kf, grad_vf, here, there = call(
        back_kernel,
        [WIDE_LOW, WIDE_LOW, WIDE, WIDE, STATE, PIECES],
        queries, key_input, value_input, cotangent, gain, raw, low, swap_cores(give), parts,
        own, other,
        flops=500_000_000,
    )
    chip = scan(total, True)
    there = swap_cores(chip + there)
    parts = key_input, value_input, grad_kf, grad_vf
    own = call(own_kernel, [HALF_LOW, HALF_LOW], *parts, chip, here, flops=50_000_000)
    store = [pltpu.VMEM(*HALF_LOW)] * 2 + [pltpu.SemaphoreType.DMA((4,))]
    grad_key, grad_value = call(
        last_kernel,
        [WIDE_LOW, WIDE_LOW],
        *parts, there, *own,
        out_space=pl.BlockSpec(memory_space=pltpu.HBM),
        scratch=store,
    )
    return (attended, grad_query, grad_key, grad_value)


def solution(mesh):
    in_specs = (P("ctx", "head"), P("ctx", "head"), P("ctx", "head"), P("head"), P("ctx", "head"))
    out_specs = (P("ctx", "head"), P("ctx", "head"), P("ctx", "head"), P("ctx", "head"))
    return jax.shard_map(
        per_device, mesh=mesh, in_specs=in_specs, out_specs=out_specs, check_vma=False
    )
```

```python
import jax
import jax.numpy as jnp
from jax import lax
from jax.experimental import pallas as pl
from jax.experimental.pallas import tpu as pltpu
from jax.sharding import PartitionSpec as P

HEAD_DIM = 96
D = 6144
TOK = 128
LANES = 128
HALF_HEADS = 4
HALF = HALF_HEADS * HEAD_DIM
CHIPS = 64
CORES = 2
PIECE = 640

epsilon = 1e-06
F32 = jnp.float32
BF16 = jnp.bfloat16
VMEM = pl.BlockSpec(memory_space=pltpu.VMEM)
NN = (((1,), (0,)), ((), ()))
NT = (((1,), (1,)), ((), ()))
TN = (((0,), (0,)), ((), ()))


def mm(a, b, dims):
    return lax.dot_general(a, b, dims, preferred_element_type=F32)


def half(g):
    return slice(g * HALF, (g + 1) * HALF)


def head_masks(rows):
    lane = lax.broadcasted_iota(jnp.int32, (rows, HALF), 1)
    return [(lane >= h * HEAD_DIM) & (lane < (h + 1) * HEAD_DIM) for h in range(HALF_HEADS)]


def spread(x):
    return jnp.concatenate([x * m.astype(BF16) for m in head_masks(x.shape[0])], axis=0)


def diagonal(x):
    rows = x.shape[0] // HALF_HEADS
    masks = head_masks(rows)
    out = x[:rows]
    for h in range(1, HALF_HEADS):
        out = jnp.where(masks[h], x[h * rows : (h + 1) * rows], out)
    return out


def to_pieces(state):
    rest = state[64:96]
    tail = rest[:, 256:384]
    return jnp.concatenate(
        [
            state[0:64],
            jnp.concatenate([rest[:, 0:128], rest[:, 128:256]], axis=0),
            jnp.concatenate([tail, pltpu.roll(tail, 64, 1)], axis=0),
        ],
        axis=1,
    )


def from_pieces(pieces):
    low = lax.broadcasted_iota(jnp.int32, (32, LANES), 1) < 64
    tail = jnp.where(low, pieces[0:32, 512:640], pltpu.roll(pieces[32:64, 512:640], 64, 1))
    rest = jnp.concatenate([pieces[0:32, 384:512], pieces[32:64, 384:512], tail], axis=1)
    return jnp.concatenate([pieces[:, 0:384], rest], axis=0)


def silu_low(x):
    x = x.astype(F32)
    return (x * jax.nn.sigmoid(x)).astype(BF16)


def silu_slope(x):
    x = x.astype(F32)
    sig = jax.nn.sigmoid(x)
    return sig * (1.0 + x * (1.0 - sig))


def causal4():
    row = lax.broadcasted_iota(jnp.int32, (TOK, TOK), 0)
    col = lax.broadcasted_iota(jnp.int32, (TOK, TOK), 1)
    keep = jnp.where(row >= col, 1.0, 0.0)
    return jnp.concatenate([keep] * HALF_HEADS, axis=1) > 0.5


def by_head(x):
    return jnp.concatenate([x[:, h * TOK : (h + 1) * TOK] for h in range(HALF_HEADS)], axis=0)


def core_index():
    return lax.axis_index("ctx") % CORES


def pick(own, x):
    first = (core_index() == 0) == own
    return jnp.where(first, x[:, half(0)], x[:, half(1)])


def in_order(own, other):
    first = core_index() == 0
    return jnp.where(first, own, other), jnp.where(first, other, own)


def state_kernel(pair_ref, mine_ref, theirs_ref):
    first, second = (
        to_pieces(diagonal(mm(silu_low(pair_ref[0, :, half(g)]), pair_ref[1, :, half(g)], TN)))
        for g in range(CORES)
    )
    low = core_index() == 0
    mine_ref[:, 0, :] = jnp.where(low, first, second)
    theirs_ref[:, 0, :] = jnp.where(low, second, first)


def send_kernel(q_ref, k_ref, v_ref, c_ref, out_ref):
    for i, ref in enumerate((q_ref, k_ref, v_ref, c_ref)):
        out_ref[i] = pick(False, ref[...]).astype(F32)


def attention(q_feat, k_feat):
    return jnp.where(causal4(), mm(q_feat, spread(k_feat), NT), 0.0).astype(BF16)


def intra_kernel(q_ref, k_ref, v_ref, got_ref, intra_ref, done_ref):
    done_ref[...] = jnp.zeros_like(done_ref)
    mine = [pick(True, ref[...]) for ref in (q_ref, k_ref, v_ref)]
    others = [got_ref[i].astype(BF16) for i in range(3)]
    for i, (q, k, v) in enumerate((mine, others)):
        intra_ref[i] = mm(attention(silu_low(q), silu_low(k)), spread(v), NN)


def scan_kernel(backward, pieces_ref, *refs):
    out_ref = refs[-1]
    total = jnp.zeros((1, PIECE), F32)
    for i in range(CHIPS):
        chip = CHIPS - 1 - i if backward else i
        out_ref[chip] = total
        total = total + pieces_ref[chip]


def lane_sums(x):
    part = x[:, 0:LANES]
    for i in range(1, x.shape[1] // LANES):
        part = part + x[:, i * LANES : (i + 1) * LANES]
    return jnp.sum(part.T, axis=0, keepdims=True)


def raw_kernel(
    q_ref, c_ref, gain_ref, got_ref, intra_ref, chip_ref, mine_ref, received_ref,
    raw_ref, low_ref, give_ref, parts_ref,
):
    core = core_index()
    chip = chip_ref[:, 0, :]
    own = from_pieces(chip + jnp.where(core == 1, received_ref[:, 0, :], 0.0))
    other = from_pieces(chip + jnp.where(core == 0, mine_ref[:, 0, :], 0.0))
    low_ref[...] = own.astype(BF16)
    give_ref[TOK:, :] = other
    gain = pick(True, gain_ref[...])
    q, c = pick(True, q_ref[...]), pick(True, c_ref[...])
    sums = []
    for i, (q, c, state) in enumerate(
        ((q, c, own), (got_ref[0].astype(BF16), got_ref[3], other))
    ):
        raw = intra_ref[i] + mm(silu_low(q), spread(state.astype(BF16)), NN)
        raw_ref[i] = raw
        upstream = c.astype(F32) * gain
        sums.append(jnp.concatenate([lane_sums(raw * raw), lane_sums(upstream * raw)], axis=0))
    give_ref[0:TOK, :] = raw_ref[1]
    sums = jnp.concatenate(in_order(*sums), axis=0)
    parts_ref[...] = jnp.broadcast_to(sums[None], parts_ref.shape)


def scales(totals):
    square = jnp.broadcast_to(totals[0:1], (TOK, LANES)).T
    cross = jnp.broadcast_to(totals[1:2], (TOK, LANES)).T
    mean = square * (1.0 / D) + epsilon
    pair = lax.rsqrt(mean), cross / (D * mean)
    return [jnp.concatenate([x] * (HALF // LANES), axis=1) for x in pair]


def gradient(c, gain, raw, inverse, pull):
    return ((c.astype(F32) * gain - raw * pull) * inverse).astype(BF16)


def own_and_other(parts_ref):
    totals = jnp.sum(parts_ref[...], axis=0)
    return in_order(totals[0:2], totals[2:4])


def grad_state_kernel(
    q_ref, c_ref, gain_ref, got_ref, raw_ref, parts_ref, sum_ref, own_ref, other_ref
):
    gain = pick(True, gain_ref[...])
    q, c = pick(True, q_ref[...]), pick(True, c_ref[...])
    states = []
    for i, (q, c, totals) in enumerate(
        zip((q, got_ref[0].astype(BF16)), (c, got_ref[3]), own_and_other(parts_ref))
    ):
        d_raw = gradient(c, gain, raw_ref[i], *scales(totals))
        states.append(diagonal(mm(silu_low(q), d_raw, TN)))
    own_ref[...], other_ref[...] = states
    sum_ref[:, 0, :] = to_pieces(states[0] + states[1])


def back_kernel(
    q_ref, k_ref, v_ref, c_ref, gain_ref, raw_ref, low_ref, got_ref, parts_ref, own_ref, other_ref,
    attended_ref, grad_q_ref, grad_kf_ref, grad_vf_ref, k_feat_ref, slope_ref, here_ref, there_ref,
):
    core = core_index()
    here_ref[...] = jnp.where(core == 0, other_ref[...], 0.0)
    there_ref[:, 0, :] = to_pieces(jnp.where(core == 1, own_ref[...], 0.0))
    keep = causal4()
    inverse, pull = scales(own_and_other(parts_ref)[0])
    raws = in_order(raw_ref[0], got_ref[0:TOK])
    lows = in_order(low_ref[...].astype(F32), got_ref[TOK:])
    for g in range(CORES):
        q, raw, gain = q_ref[:, half(g)], raws[g], gain_ref[:, half(g)]
        q_feat, k_feat = silu_low(q), silu_low(k_ref[:, half(g)])
        k_feat_ref[:, half(g)] = k_feat
        slope_ref[:, half(g)] = silu_slope(k_ref[:, half(g)])
        attended_ref[:, half(g)] = (raw * inverse * gain).astype(BF16)
        d_raw = gradient(c_ref[:, half(g)], gain, raw, inverse, pull)
        back = jnp.where(keep, mm(d_raw, spread(v_ref[:, half(g)]), NT), 0.0).astype(BF16)
        grad_qf = mm(back, spread(k_feat), NN) + mm(d_raw, spread(lows[g].astype(BF16)), NT)
        grad_q_ref[:, half(g)] = (grad_qf * silu_slope(q)).astype(BF16)
        grad_kf_ref[:, half(g)] = mm(by_head(back), spread(q_feat), TN)
        grad_vf_ref[:, half(g)] = mm(by_head(attention(q_feat, k_feat)), spread(d_raw), TN)


def key_gradient(own, v_ref, slope_ref, grad_kf_ref, later):
    v, slope, grad_kf = (pick(own, ref[...]) for ref in (v_ref, slope_ref, grad_kf_ref))
    return ((grad_kf + mm(v, later, NT)) * slope).astype(BF16)


def value_gradient(own, k_feat_ref, grad_vf_ref, later):
    k_feat, grad_vf = pick(own, k_feat_ref[...]), pick(own, grad_vf_ref[...])
    return (grad_vf + mm(k_feat, later, NN)).astype(BF16)


def own_kernel(
    v_ref, k_feat_ref, slope_ref, grad_kf_ref, grad_vf_ref, chip_ref, here_ref, grad_k_ref, grad_v_ref
):
    later = spread((from_pieces(chip_ref[:, 0, :]) + here_ref[...]).astype(BF16))
    grad_k_ref[...] = key_gradient(True, v_ref, slope_ref, grad_kf_ref, later)
    grad_v_ref[...] = value_gradient(True, k_feat_ref, grad_vf_ref, later)


def last_kernel(
    v_ref, k_feat_ref, slope_ref, grad_kf_ref, grad_vf_ref, there_ref, own_k_ref, own_v_ref,
    grad_k_hbm, grad_v_hbm, other_k_ref, other_v_ref, sems,
):
    core = core_index()
    own = pl.ds(pl.multiple_of(core * HALF, HALF), HALF)
    other = pl.ds(pl.multiple_of((1 - core) * HALF, HALF), HALF)
    copies = [
        pltpu.make_async_copy(own_k_ref, grad_k_hbm.at[:, own], sems.at[0]),
        pltpu.make_async_copy(own_v_ref, grad_v_hbm.at[:, own], sems.at[1]),
        pltpu.make_async_copy(other_k_ref, grad_k_hbm.at[:, other], sems.at[2]),
        pltpu.make_async_copy(other_v_ref, grad_v_hbm.at[:, other], sems.at[3]),
    ]
    copies[0].start()
    copies[1].start()
    later = spread(from_pieces(there_ref[:, 0, :]).astype(BF16))
    other_k_ref[...] = key_gradient(False, v_ref, slope_ref, grad_kf_ref, later)
    copies[2].start()
    other_v_ref[...] = value_gradient(False, k_feat_ref, grad_vf_ref, later)
    copies[3].start()
    for copy in copies:
        copy.wait()


def call(kernel, outs, *args, flops=0, out_space=VMEM, scratch=()):
    return pl.pallas_call(
        kernel,
        out_shape=[jax.ShapeDtypeStruct(shape, kind) for shape, kind in outs],
        in_specs=[VMEM] * len(args),
        out_specs=[out_space] * len(outs),
        scratch_shapes=list(scratch),
        compiler_params=pltpu.CompilerParams(vmem_limit_bytes=32 * 1024 * 1024),
        cost_estimate=pl.CostEstimate(flops=flops, bytes_accessed=1_000_000, transcendentals=0),
    )(*args)


def swap_cores(x):
    pairs = [(i, i ^ 1) for i in range(CHIPS * CORES)]
    return lax.ppermute(x, "ctx", pairs)


def across_chips(x):
    groups = [[chip * CORES + core for chip in range(CHIPS)] for core in range(CORES)]
    return lax.all_to_all(x, "ctx", 0, 0, axis_index_groups=groups)


def over_heads(x):
    size = CORES * lax.axis_size("head")
    groups = [[chip * size + i for i in range(size)] for chip in range(CHIPS)]
    return lax.all_to_all(x, ("ctx", "head"), 0, 0, axis_index_groups=groups)


PIECES = ((CHIPS, 1, PIECE), F32)
WIDE = ((TOK, CORES * HALF), F32)
WIDE_LOW = ((TOK, CORES * HALF), BF16)
DONE = ((8, LANES), F32)
STATE = ((HEAD_DIM, HALF), F32)
HALF_LOW = ((TOK, HALF), BF16)
BLOCKS = ((CORES, TOK, HALF), F32)


def scan(pieces, backward, *after):
    def kernel(*refs):
        scan_kernel(backward, *refs)

    (summed,) = call(kernel, [PIECES], across_chips(pieces), *after)
    return across_chips(summed)


def per_device(queries, key_input, value_input, norm_gain, cotangent):
    sharers = CORES * lax.axis_size("head")
    gain = norm_gain.reshape(1, -1)
    mine, theirs = call(state_kernel, [PIECES, PIECES], jnp.stack([key_input, value_input]))
    received = swap_cores(theirs)
    (given,) = call(
        send_kernel, [((4, TOK, HALF), F32)], queries, key_input, value_input, cotangent
    )
    got = swap_cores(given)
    intra, done = call(
        intra_kernel, [BLOCKS, DONE], queries, key_input, value_input, got, flops=200_000_000
    )
    chip = scan(mine + received, False, done)
    raw, low, give, parts = call(
        raw_kernel,
        [BLOCKS, ((HEAD_DIM, HALF), BF16), ((TOK + HEAD_DIM, HALF), F32), ((sharers, 4, TOK), F32)],
        queries, cotangent, gain, got, intra, chip, mine, received,
    )
    parts = over_heads(parts)
    total, own, other = call(
        grad_state_kernel,
        [PIECES, STATE, STATE],
        queries, cotangent, gain, got, raw, parts,
    )
    attended, grad_query, grad_kf, grad_vf, k_feat, slope, here, there = call(
        back_kernel,
        [WIDE_LOW, WIDE_LOW, WIDE, WIDE, WIDE_LOW, WIDE, STATE, PIECES],
        queries, key_input, value_input, cotangent, gain, raw, low, swap_cores(give), parts,
        own, other,
        flops=500_000_000,
    )
    chip = scan(total, True)
    there = swap_cores(chip + there)
    parts = value_input, k_feat, slope, grad_kf, grad_vf
    own = call(own_kernel, [HALF_LOW, HALF_LOW], *parts, chip, here, flops=50_000_000)
    store = [pltpu.VMEM(*HALF_LOW)] * 2 + [pltpu.SemaphoreType.DMA((4,))]
    grad_key, grad_value = call(
        last_kernel,
        [WIDE_LOW, WIDE_LOW],
        *parts, there, *own,
        out_space=pl.BlockSpec(memory_space=pltpu.HBM),
        scratch=store,
    )
    return (attended, grad_query, grad_key, grad_value)


def solution(mesh):
    in_specs = (P("ctx", "head"), P("ctx", "head"), P("ctx", "head"), P("head"), P("ctx", "head"))
    out_specs = (P("ctx", "head"), P("ctx", "head"), P("ctx", "head"), P("ctx", "head"))
    return jax.shard_map(
        per_device, mesh=mesh, in_specs=in_specs, out_specs=out_specs, check_vma=False
    )
```

```python
import jax
import jax.numpy as jnp
from jax import lax
from jax.experimental import pallas as pl
from jax.experimental.pallas import tpu as pltpu
from jax.sharding import PartitionSpec as P

HEAD_DIM = 96
D = 6144
TOK = 128
LANES = 128
HALF_HEADS = 4
HALF = HALF_HEADS * HEAD_DIM
CHIPS = 64
CORES = 2
PIECE = 640

epsilon = 1e-06
F32 = jnp.float32
BF16 = jnp.bfloat16
VMEM = pl.BlockSpec(memory_space=pltpu.VMEM)
NN = (((1,), (0,)), ((), ()))
NT = (((1,), (1,)), ((), ()))
TN = (((0,), (0,)), ((), ()))


def mm(a, b, dims):
    return lax.dot_general(a, b, dims, preferred_element_type=F32)


def half(g):
    return slice(g * HALF, (g + 1) * HALF)


def head_masks(rows):
    lane = lax.broadcasted_iota(jnp.int32, (rows, HALF), 1)
    return [(lane >= h * HEAD_DIM) & (lane < (h + 1) * HEAD_DIM) for h in range(HALF_HEADS)]


def spread(x):
    return jnp.concatenate([x * m.astype(BF16) for m in head_masks(x.shape[0])], axis=0)


def diagonal(x):
    rows = x.shape[0] // HALF_HEADS
    masks = head_masks(rows)
    out = x[:rows]
    for h in range(1, HALF_HEADS):
        out = jnp.where(masks[h], x[h * rows : (h + 1) * rows], out)
    return out


def to_pieces(state):
    rest = state[64:96]
    tail = rest[:, 256:384]
    return jnp.concatenate(
        [
            state[0:64],
            jnp.concatenate([rest[:, 0:128], rest[:, 128:256]], axis=0),
            jnp.concatenate([tail, pltpu.roll(tail, 64, 1)], axis=0),
        ],
        axis=1,
    )


def from_pieces(pieces):
    low = lax.broadcasted_iota(jnp.int32, (32, LANES), 1) < 64
    tail = jnp.where(low, pieces[0:32, 512:640], pltpu.roll(pieces[32:64, 512:640], 64, 1))
    rest = jnp.concatenate([pieces[0:32, 384:512], pieces[32:64, 384:512], tail], axis=1)
    return jnp.concatenate([pieces[:, 0:384], rest], axis=0)


def silu_low(x):
    x = x.astype(F32)
    return (x * jax.nn.sigmoid(x)).astype(BF16)


def silu_slope(x):
    x = x.astype(F32)
    sig = jax.nn.sigmoid(x)
    return sig * (1.0 + x * (1.0 - sig))


def causal4():
    row = lax.broadcasted_iota(jnp.int32, (TOK, TOK), 0)
    col = lax.broadcasted_iota(jnp.int32, (TOK, TOK), 1)
    keep = jnp.where(row >= col, 1.0, 0.0)
    return jnp.concatenate([keep] * HALF_HEADS, axis=1) > 0.5


def by_head(x):
    return jnp.concatenate([x[:, h * TOK : (h + 1) * TOK] for h in range(HALF_HEADS)], axis=0)


def core_index():
    return lax.axis_index("ctx") % CORES


def pick(own, x):
    first = (core_index() == 0) == own
    return jnp.where(first, x[:, half(0)], x[:, half(1)])


def in_order(own, other):
    first = core_index() == 0
    return jnp.where(first, own, other), jnp.where(first, other, own)


def state_kernel(pair_ref, mine_ref, theirs_ref):
    first, second = (
        to_pieces(diagonal(mm(silu_low(pair_ref[0, :, half(g)]), pair_ref[1, :, half(g)], TN)))
        for g in range(CORES)
    )
    low = core_index() == 0
    mine_ref[:, 0, :] = jnp.where(low, first, second)
    theirs_ref[:, 0, :] = jnp.where(low, second, first)


def send_kernel(after_ref, q_ref, k_ref, v_ref, c_ref, qc_ref, kv_ref):
    for out_ref, refs in ((qc_ref, (q_ref, c_ref)), (kv_ref, (k_ref, v_ref))):
        for i, ref in enumerate(refs):
            out_ref[i] = pick(False, ref[...]).astype(F32)


def attention(q_feat, k_feat):
    return jnp.where(causal4(), mm(q_feat, spread(k_feat), NT), 0.0).astype(BF16)


def intra_kernel(q_ref, k_ref, v_ref, got_qc_ref, got_kv_ref, intra_ref):
    mine = [pick(True, ref[...]) for ref in (q_ref, k_ref, v_ref)]
    others = [x.astype(BF16) for x in (got_qc_ref[0], got_kv_ref[0], got_kv_ref[1])]
    for i, (q, k, v) in enumerate((mine, others)):
        intra_ref[i] = mm(attention(silu_low(q), silu_low(k)), spread(v), NN)


def scan_kernel(backward, pieces_ref, out_ref, *done):
    for ref in done:
        ref[...] = jnp.zeros_like(ref)
    total = jnp.zeros((1, PIECE), F32)
    for i in range(CHIPS):
        chip = CHIPS - 1 - i if backward else i
        out_ref[chip] = total
        total = total + pieces_ref[chip]


def lane_sums(x):
    part = x[:, 0:LANES]
    for i in range(1, x.shape[1] // LANES):
        part = part + x[:, i * LANES : (i + 1) * LANES]
    return jnp.sum(part.T, axis=0, keepdims=True)


def raw_kernel(
    q_ref, c_ref, gain_ref, got_ref, intra_ref, chip_ref, mine_ref, received_ref,
    raw_ref, low_ref, give_ref, parts_ref,
):
    core = core_index()
    chip = chip_ref[:, 0, :]
    own = from_pieces(chip + jnp.where(core == 1, received_ref[:, 0, :], 0.0))
    other = from_pieces(chip + jnp.where(core == 0, mine_ref[:, 0, :], 0.0))
    low_ref[...] = own.astype(BF16)
    give_ref[TOK:, :] = other
    gain = pick(True, gain_ref[...])
    q, c = pick(True, q_ref[...]), pick(True, c_ref[...])
    sums = []
    for i, (q, c, state) in enumerate(
        ((q, c, own), (got_ref[0].astype(BF16), got_ref[1], other))
    ):
        raw = intra_ref[i] + mm(silu_low(q), spread(state.astype(BF16)), NN)
        raw_ref[i] = raw
        upstream = c.astype(F32) * gain
        sums.append(jnp.concatenate([lane_sums(raw * raw), lane_sums(upstream * raw)], axis=0))
    give_ref[0:TOK, :] = raw_ref[1]
    sums = jnp.concatenate(in_order(*sums), axis=0)
    parts_ref[...] = jnp.broadcast_to(sums[None], parts_ref.shape)


def scales(totals):
    square = jnp.broadcast_to(totals[0:1], (TOK, LANES)).T
    cross = jnp.broadcast_to(totals[1:2], (TOK, LANES)).T
    mean = square * (1.0 / D) + epsilon
    pair = lax.rsqrt(mean), cross / (D * mean)
    return [jnp.concatenate([x] * (HALF // LANES), axis=1) for x in pair]


def gradient(c, gain, raw, inverse, pull):
    return ((c.astype(F32) * gain - raw * pull) * inverse).astype(BF16)


def own_and_other(parts_ref):
    totals = jnp.sum(parts_ref[...], axis=0)
    return in_order(totals[0:2], totals[2:4])


def grad_state_kernel(
    q_ref, c_ref, gain_ref, got_ref, raw_ref, parts_ref, sum_ref, own_ref, other_ref
):
    gain = pick(True, gain_ref[...])
    q, c = pick(True, q_ref[...]), pick(True, c_ref[...])
    states = []
    for i, (q, c, totals) in enumerate(
        zip((q, got_ref[0].astype(BF16)), (c, got_ref[1]), own_and_other(parts_ref))
    ):
        d_raw = gradient(c, gain, raw_ref[i], *scales(totals))
        states.append(diagonal(mm(silu_low(q), d_raw, TN)))
    own_ref[...], other_ref[...] = states
    sum_ref[:, 0, :] = to_pieces(states[0] + states[1])


def back_kernel(
    q_ref, k_ref, v_ref, c_ref, gain_ref, raw_ref, low_ref, got_ref, parts_ref, own_ref, other_ref,
    attended_ref, grad_q_ref, grad_kf_ref, grad_vf_ref, here_ref, there_ref,
):
    core = core_index()
    here_ref[...] = jnp.where(core == 0, other_ref[...], 0.0)
    there_ref[:, 0, :] = to_pieces(jnp.where(core == 1, own_ref[...], 0.0))
    keep = causal4()
    inverse, pull = scales(own_and_other(parts_ref)[0])
    raws = in_order(raw_ref[0], got_ref[0:TOK])
    lows = in_order(low_ref[...].astype(F32), got_ref[TOK:])
    for g in range(CORES):
        q, raw, gain = q_ref[:, half(g)], raws[g], gain_ref[:, half(g)]
        q_feat, k_feat = silu_low(q), silu_low(k_ref[:, half(g)])
        attended_ref[:, half(g)] = (raw * inverse * gain).astype(BF16)
        d_raw = gradient(c_ref[:, half(g)], gain, raw, inverse, pull)
        back = jnp.where(keep, mm(d_raw, spread(v_ref[:, half(g)]), NT), 0.0).astype(BF16)
        grad_qf = mm(back, spread(k_feat), NN) + mm(d_raw, spread(lows[g].astype(BF16)), NT)
        grad_q_ref[:, half(g)] = (grad_qf * silu_slope(q)).astype(BF16)
        grad_kf_ref[:, half(g)] = mm(by_head(back), spread(q_feat), TN)
        grad_vf_ref[:, half(g)] = mm(by_head(attention(q_feat, k_feat)), spread(d_raw), TN)


def finished(own, refs, later):
    k, v, grad_kf, grad_vf = (pick(own, ref[...]) for ref in refs)
    later = spread(later.astype(BF16))
    grad_k = (grad_kf + mm(v, later, NT)) * silu_slope(k)
    return grad_k.astype(BF16), (grad_vf + mm(silu_low(k), later, NN)).astype(BF16)


def own_kernel(
    k_ref, v_ref, grad_kf_ref, grad_vf_ref, chip_ref, here_ref, grad_k_ref, grad_v_ref
):
    later = from_pieces(chip_ref[:, 0, :]) + here_ref[...]
    refs = k_ref, v_ref, grad_kf_ref, grad_vf_ref
    grad_k_ref[...], grad_v_ref[...] = finished(True, refs, later)


def last_kernel(
    k_ref, v_ref, grad_kf_ref, grad_vf_ref, there_ref, own_k_ref, own_v_ref,
    grad_k_hbm, grad_v_hbm, other_k_ref, other_v_ref, sems,
):
    core = core_index()
    own = pl.ds(pl.multiple_of(core * HALF, HALF), HALF)
    other = pl.ds(pl.multiple_of((1 - core) * HALF, HALF), HALF)
    copies = [
        pltpu.make_async_copy(own_k_ref, grad_k_hbm.at[:, own], sems.at[0]),
        pltpu.make_async_copy(own_v_ref, grad_v_hbm.at[:, own], sems.at[1]),
        pltpu.make_async_copy(other_k_ref, grad_k_hbm.at[:, other], sems.at[2]),
        pltpu.make_async_copy(other_v_ref, grad_v_hbm.at[:, other], sems.at[3]),
    ]
    copies[0].start()
    copies[1].start()
    refs = k_ref, v_ref, grad_kf_ref, grad_vf_ref
    later = from_pieces(there_ref[:, 0, :])
    other_k_ref[...], other_v_ref[...] = finished(False, refs, later)
    copies[2].start()
    copies[3].start()
    for copy in copies:
        copy.wait()


def call(kernel, outs, *args, flops=0, out_space=VMEM, scratch=()):
    return pl.pallas_call(
        kernel,
        out_shape=[jax.ShapeDtypeStruct(shape, kind) for shape, kind in outs],
        in_specs=[VMEM] * len(args),
        out_specs=[out_space] * len(outs),
        scratch_shapes=list(scratch),
        compiler_params=pltpu.CompilerParams(vmem_limit_bytes=32 * 1024 * 1024),
        cost_estimate=pl.CostEstimate(flops=flops, bytes_accessed=1_000_000, transcendentals=0),
    )(*args)


def swap_cores(x):
    pairs = [(i, i ^ 1) for i in range(CHIPS * CORES)]
    return lax.ppermute(x, "ctx", pairs)


def across_chips(x):
    groups = [[chip * CORES + core for chip in range(CHIPS)] for core in range(CORES)]
    return lax.all_to_all(x, "ctx", 0, 0, axis_index_groups=groups)


def over_heads(x):
    size = CORES * lax.axis_size("head")
    groups = [[chip * size + i for i in range(size)] for chip in range(CHIPS)]
    return lax.all_to_all(x, ("ctx", "head"), 0, 0, axis_index_groups=groups)


PIECES = ((CHIPS, 1, PIECE), F32)
WIDE = ((TOK, CORES * HALF), F32)
WIDE_LOW = ((TOK, CORES * HALF), BF16)
STATE = ((HEAD_DIM, HALF), F32)
HALF_LOW = ((TOK, HALF), BF16)
BLOCKS = ((CORES, TOK, HALF), F32)


def scan(pieces, backward):
    def kernel(*refs):
        scan_kernel(backward, *refs)

    done = [] if backward else [((8, LANES), F32)]
    summed, *done = call(kernel, [PIECES] + done, across_chips(pieces))
    return across_chips(summed), *done


def per_device(queries, key_input, value_input, norm_gain, cotangent):
    sharers = CORES * lax.axis_size("head")
    gain = norm_gain.reshape(1, -1)
    mine, theirs = call(state_kernel, [PIECES, PIECES], jnp.stack([key_input, value_input]))
    received = swap_cores(theirs)
    chip, done = scan(mine + received, False)
    halves = call(
        send_kernel,
        [((2, TOK, HALF), F32)] * 2,
        done, queries, key_input, value_input, cotangent,
    )
    got, got_kv = (swap_cores(x) for x in halves)
    (intra,) = call(
        intra_kernel,
        [BLOCKS],
        queries, key_input, value_input, got, got_kv,
        flops=200_000_000,
    )
    raw, low, give, parts = call(
        raw_kernel,
        [BLOCKS, ((HEAD_DIM, HALF), BF16), ((TOK + HEAD_DIM, HALF), F32), ((sharers, 4, TOK), F32)],
        queries, cotangent, gain, got, intra, chip, mine, received,
    )
    parts = over_heads(parts)
    total, own, other = call(
        grad_state_kernel,
        [PIECES, STATE, STATE],
        queries, cotangent, gain, got, raw, parts,
    )
    attended, grad_query, grad_kf, grad_vf, here, there = call(
        back_kernel,
        [WIDE_LOW, WIDE_LOW, WIDE, WIDE, STATE, PIECES],
        queries, key_input, value_input, cotangent, gain, raw, low, swap_cores(give), parts,
        own, other,
        flops=500_000_000,
    )
    (chip,) = scan(total, True)
    there = swap_cores(chip + there)
    parts = key_input, value_input, grad_kf, grad_vf
    own = call(own_kernel, [HALF_LOW, HALF_LOW], *parts, chip, here, flops=50_000_000)
    store = [pltpu.VMEM(*HALF_LOW)] * 2 + [pltpu.SemaphoreType.DMA((4,))]
    grad_key, grad_value = call(
        last_kernel,
        [WIDE_LOW, WIDE_LOW],
        *parts, there, *own,
        out_space=pl.BlockSpec(memory_space=pltpu.HBM),
        scratch=store,
    )
    return (attended, grad_query, grad_key, grad_value)


def solution(mesh):
    in_specs = (P("ctx", "head"), P("ctx", "head"), P("ctx", "head"), P("head"), P("ctx", "head"))
    out_specs = (P("ctx", "head"), P("ctx", "head"), P("ctx", "head"), P("ctx", "head"))
    return jax.shard_map(
        per_device, mesh=mesh, in_specs=in_specs, out_specs=out_specs, check_vma=False
    )
```

```python
import functools

import jax
import jax.numpy as jnp
from jax import lax
from jax.experimental import pallas as pl
from jax.experimental.pallas import tpu as pltpu
from jax.sharding import PartitionSpec as P

HEAD_DIM = 96
D = 6144
TOK = 128
LANES = 128
HALF_HEADS = 4
HALF = HALF_HEADS * HEAD_DIM
CHIPS = 64
CORES = 2
PIECE = 640
PARTS = 4
PART = CHIPS // PARTS

epsilon = 1e-06
F32 = jnp.float32
BF16 = jnp.bfloat16
VMEM = pl.BlockSpec(memory_space=pltpu.VMEM)
NN = (((1,), (0,)), ((), ()))
NT = (((1,), (1,)), ((), ()))
TN = (((0,), (0,)), ((), ()))


def mm(a, b, dims):
    return lax.dot_general(a, b, dims, preferred_element_type=F32)


def half(g):
    return slice(g * HALF, (g + 1) * HALF)


def head_masks(rows):
    lane = lax.broadcasted_iota(jnp.int32, (rows, HALF), 1)
    return [(lane >= h * HEAD_DIM) & (lane < (h + 1) * HEAD_DIM) for h in range(HALF_HEADS)]


def spread(x):
    return jnp.concatenate([x * m.astype(BF16) for m in head_masks(x.shape[0])], axis=0)


def diagonal(x):
    rows = x.shape[0] // HALF_HEADS
    masks = head_masks(rows)
    out = x[:rows]
    for h in range(1, HALF_HEADS):
        out = jnp.where(masks[h], x[h * rows : (h + 1) * rows], out)
    return out


def to_pieces(state):
    rest = state[64:96]
    tail = rest[:, 256:384]
    return jnp.concatenate(
        [
            state[0:64],
            jnp.concatenate([rest[:, 0:128], rest[:, 128:256]], axis=0),
            jnp.concatenate([tail, pltpu.roll(tail, 64, 1)], axis=0),
        ],
        axis=1,
    )


def from_pieces(pieces):
    low = lax.broadcasted_iota(jnp.int32, (32, LANES), 1) < 64
    tail = jnp.where(low, pieces[0:32, 512:640], pltpu.roll(pieces[32:64, 512:640], 64, 1))
    rest = jnp.concatenate([pieces[0:32, 384:512], pieces[32:64, 384:512], tail], axis=1)
    return jnp.concatenate([pieces[:, 0:384], rest], axis=0)


def silu_low(x):
    x = x.astype(F32)
    return (x * jax.nn.sigmoid(x)).astype(BF16)


def silu_slope(x):
    x = x.astype(F32)
    sig = jax.nn.sigmoid(x)
    return sig * (1.0 + x * (1.0 - sig))


def causal4():
    row = lax.broadcasted_iota(jnp.int32, (TOK, TOK), 0)
    col = lax.broadcasted_iota(jnp.int32, (TOK, TOK), 1)
    keep = jnp.where(row >= col, 1.0, 0.0)
    return jnp.concatenate([keep] * HALF_HEADS, axis=1) > 0.5


def by_head(x):
    return jnp.concatenate([x[:, h * TOK : (h + 1) * TOK] for h in range(HALF_HEADS)], axis=0)


def core_index():
    return lax.axis_index("ctx") % CORES


def pick(own, x):
    first = (core_index() == 0) == own
    return jnp.where(first, x[:, half(0)], x[:, half(1)])


def in_order(own, other):
    first = core_index() == 0
    return jnp.where(first, own, other), jnp.where(first, other, own)


def state_kernel(own, pair_ref, out_ref):
    k, v = pick(own, pair_ref[0]), pick(own, pair_ref[1])
    out_ref[:, 0, :] = to_pieces(diagonal(mm(silu_low(k), v, TN)))


def send_kernel(after_ref, q_ref, k_ref, v_ref, c_ref, qc_ref, kv_ref):
    for out_ref, refs in ((qc_ref, (q_ref, c_ref)), (kv_ref, (k_ref, v_ref))):
        for i, ref in enumerate(refs):
            out_ref[i] = pick(False, ref[...]).astype(F32)


def attention(q_feat, k_feat):
    return jnp.where(causal4(), mm(q_feat, spread(k_feat), NT), 0.0).astype(BF16)


def intra_kernel(q_ref, k_ref, v_ref, got_qc_ref, got_kv_ref, intra_ref):
    mine = [pick(True, ref[...]) for ref in (q_ref, k_ref, v_ref)]
    others = [x.astype(BF16) for x in (got_qc_ref[0], got_kv_ref[0], got_kv_ref[1])]
    for i, (q, k, v) in enumerate((mine, others)):
        intra_ref[i] = mm(attention(silu_low(q), silu_low(k)), spread(v), NN)


def scan_kernel(backward, pieces_ref, out_hbm, *refs):
    *done, rows_ref, sems = refs
    total = jnp.zeros((1, PIECE), F32)
    copies = []
    for part in range(PARTS):
        first = (PARTS - 1 - part if backward else part) * PART
        for i in range(PART):
            chip = first + (PART - 1 - i if backward else i)
            rows_ref[chip] = total
            total = total + pieces_ref[chip]
        rows = pl.ds(first, PART)
        copy = pltpu.make_async_copy(rows_ref.at[rows], out_hbm.at[rows], sems.at[part])
        copy.start()
        copies.append(copy)
    for ref in done:
        ref[...] = jnp.zeros_like(ref)
    for copy in copies:
        copy.wait()


def lane_sums(x):
    part = x[:, 0:LANES]
    for i in range(1, x.shape[1] // LANES):
        part = part + x[:, i * LANES : (i + 1) * LANES]
    return jnp.sum(part.T, axis=0, keepdims=True)


def raw_kernel(
    q_ref, c_ref, gain_ref, got_ref, intra_ref, chip_ref, mine_ref, received_ref,
    raw_ref, low_ref, give_ref, parts_ref,
):
    core = core_index()
    chip = chip_ref[:, 0, :]
    own = from_pieces(chip + jnp.where(core == 1, received_ref[:, 0, :], 0.0))
    other = from_pieces(chip + jnp.where(core == 0, mine_ref[:, 0, :], 0.0))
    low_ref[...] = own.astype(BF16)
    give_ref[TOK:, :] = other
    gain = pick(True, gain_ref[...])
    q, c = pick(True, q_ref[...]), pick(True, c_ref[...])
    sums = []
    for i, (q, c, state) in enumerate(
        ((q, c, own), (got_ref[0].astype(BF16), got_ref[1], other))
    ):
        raw = intra_ref[i] + mm(silu_low(q), spread(state.astype(BF16)), NN)
        raw_ref[i] = raw
        upstream = c.astype(F32) * gain
        sums.append(jnp.concatenate([lane_sums(raw * raw), lane_sums(upstream * raw)], axis=0))
    give_ref[0:TOK, :] = raw_ref[1]
    sums = jnp.concatenate(in_order(*sums), axis=0)
    parts_ref[...] = jnp.broadcast_to(sums[None], parts_ref.shape)


def scales(totals):
    square = jnp.broadcast_to(totals[0:1], (TOK, LANES)).T
    cross = jnp.broadcast_to(totals[1:2], (TOK, LANES)).T
    mean = square * (1.0 / D) + epsilon
    pair = lax.rsqrt(mean), cross / (D * mean)
    return [jnp.concatenate([x] * (HALF // LANES), axis=1) for x in pair]


def gradient(c, gain, raw, inverse, pull):
    return ((c.astype(F32) * gain - raw * pull) * inverse).astype(BF16)


def own_and_other(parts_ref):
    totals = jnp.sum(parts_ref[...], axis=0)
    return in_order(totals[0:2], totals[2:4])


def grad_state_kernel(
    q_ref, c_ref, gain_ref, got_ref, raw_ref, parts_ref, sum_ref, own_ref, other_ref
):
    gain = pick(True, gain_ref[...])
    q, c = pick(True, q_ref[...]), pick(True, c_ref[...])
    states = []
    for i, (q, c, totals) in enumerate(
        zip((q, got_ref[0].astype(BF16)), (c, got_ref[1]), own_and_other(parts_ref))
    ):
        d_raw = gradient(c, gain, raw_ref[i], *scales(totals))
        states.append(diagonal(mm(silu_low(q), d_raw, TN)))
    own_ref[...], other_ref[...] = states
    sum_ref[:, 0, :] = to_pieces(states[0] + states[1])


def back_kernel(
    q_ref, k_ref, v_ref, c_ref, gain_ref, raw_ref, low_ref, got_ref, parts_ref, own_ref, other_ref,
    attended_ref, grad_q_ref, grad_kf_ref, grad_vf_ref, here_ref, there_ref,
):
    core = core_index()
    here_ref[...] = jnp.where(core == 0, other_ref[...], 0.0)
    there_ref[:, 0, :] = to_pieces(jnp.where(core == 1, own_ref[...], 0.0))
    keep = causal4()
    inverse, pull = scales(own_and_other(parts_ref)[0])
    raws = in_order(raw_ref[0], got_ref[0:TOK])
    lows = in_order(low_ref[...].astype(F32), got_ref[TOK:])
    for g in range(CORES):
        q, raw, gain = q_ref[:, half(g)], raws[g], gain_ref[:, half(g)]
        q_feat, k_feat = silu_low(q), silu_low(k_ref[:, half(g)])
        attended_ref[:, half(g)] = (raw * inverse * gain).astype(BF16)
        d_raw = gradient(c_ref[:, half(g)], gain, raw, inverse, pull)
        back = jnp.where(keep, mm(d_raw, spread(v_ref[:, half(g)]), NT), 0.0).astype(BF16)
        grad_qf = mm(back, spread(k_feat), NN) + mm(d_raw, spread(lows[g].astype(BF16)), NT)
        grad_q_ref[:, half(g)] = (grad_qf * silu_slope(q)).astype(BF16)
        grad_kf_ref[:, half(g)] = mm(by_head(back), spread(q_feat), TN)
        grad_vf_ref[:, half(g)] = mm(by_head(attention(q_feat, k_feat)), spread(d_raw), TN)


def finished(own, refs, later):
    k, v, grad_kf, grad_vf = (pick(own, ref[...]) for ref in refs)
    later = spread(later.astype(BF16))
    grad_k = (grad_kf + mm(v, later, NT)) * silu_slope(k)
    return grad_k.astype(BF16), (grad_vf + mm(silu_low(k), later, NN)).astype(BF16)


def own_kernel(
    k_ref, v_ref, grad_kf_ref, grad_vf_ref, chip_ref, here_ref, grad_k_ref, grad_v_ref
):
    later = from_pieces(chip_ref[:, 0, :]) + here_ref[...]
    refs = k_ref, v_ref, grad_kf_ref, grad_vf_ref
    grad_k_ref[...], grad_v_ref[...] = finished(True, refs, later)


def last_kernel(
    k_ref, v_ref, grad_kf_ref, grad_vf_ref, there_ref, own_k_ref, own_v_ref,
    grad_k_hbm, grad_v_hbm, other_k_ref, other_v_ref, sems,
):
    core = core_index()
    own = pl.ds(pl.multiple_of(core * HALF, HALF), HALF)
    other = pl.ds(pl.multiple_of((1 - core) * HALF, HALF), HALF)
    copies = [
        pltpu.make_async_copy(own_k_ref, grad_k_hbm.at[:, own], sems.at[0]),
        pltpu.make_async_copy(own_v_ref, grad_v_hbm.at[:, own], sems.at[1]),
        pltpu.make_async_copy(other_k_ref, grad_k_hbm.at[:, other], sems.at[2]),
        pltpu.make_async_copy(other_v_ref, grad_v_hbm.at[:, other], sems.at[3]),
    ]
    copies[0].start()
    copies[1].start()
    refs = k_ref, v_ref, grad_kf_ref, grad_vf_ref
    later = from_pieces(there_ref[:, 0, :])
    other_k_ref[...], other_v_ref[...] = finished(False, refs, later)
    copies[2].start()
    copies[3].start()
    for copy in copies:
        copy.wait()


def call(kernel, outs, *args, flops=0, out_spaces=None, scratch=()):
    return pl.pallas_call(
        kernel,
        out_shape=[jax.ShapeDtypeStruct(shape, kind) for shape, kind in outs],
        in_specs=[VMEM] * len(args),
        out_specs=out_spaces or [VMEM] * len(outs),
        scratch_shapes=list(scratch),
        compiler_params=pltpu.CompilerParams(vmem_limit_bytes=32 * 1024 * 1024),
        cost_estimate=pl.CostEstimate(flops=flops, bytes_accessed=1_000_000, transcendentals=0),
    )(*args)


def swap_cores(x):
    pairs = [(i, i ^ 1) for i in range(CHIPS * CORES)]
    return lax.ppermute(x, "ctx", pairs)


def across_chips(x):
    groups = [[chip * CORES + core for chip in range(CHIPS)] for core in range(CORES)]
    return lax.all_to_all(x, "ctx", 0, 0, axis_index_groups=groups)


def over_heads(x):
    size = CORES * lax.axis_size("head")
    groups = [[chip * size + i for i in range(size)] for chip in range(CHIPS)]
    return lax.all_to_all(x, ("ctx", "head"), 0, 0, axis_index_groups=groups)


PIECES = ((CHIPS, 1, PIECE), F32)
WIDE = ((TOK, CORES * HALF), F32)
WIDE_LOW = ((TOK, CORES * HALF), BF16)
STATE = ((HEAD_DIM, HALF), F32)
HALF_LOW = ((TOK, HALF), BF16)
BLOCKS = ((CORES, TOK, HALF), F32)


def scan(pieces, backward):
    def kernel(*refs):
        scan_kernel(backward, *refs)

    done = [] if backward else [((8, LANES), F32)]
    spaces = [pl.BlockSpec(memory_space=pltpu.HBM)] + [VMEM] * len(done)
    rows = [pltpu.VMEM(*PIECES), pltpu.SemaphoreType.DMA((PARTS,))]
    summed, *done = call(
        kernel, [PIECES] + done, across_chips(pieces), out_spaces=spaces, scratch=rows
    )
    return across_chips(summed), *done


def per_device(queries, key_input, value_input, norm_gain, cotangent):
    sharers = CORES * lax.axis_size("head")
    gain = norm_gain.reshape(1, -1)
    pair = jnp.stack([key_input, value_input])
    (theirs,) = call(functools.partial(state_kernel, False), [PIECES], pair)
    received = swap_cores(theirs)
    (mine,) = call(functools.partial(state_kernel, True), [PIECES], pair)
    chip, done = scan(mine + received, False)
    halves = call(
        send_kernel,
        [((2, TOK, HALF), F32)] * 2,
        done, queries, key_input, value_input, cotangent,
    )
    got, got_kv = (swap_cores(x) for x in halves)
    (intra,) = call(
        intra_kernel,
        [BLOCKS],
        queries, key_input, value_input, got, got_kv,
        flops=200_000_000,
    )
    raw, low, give, parts = call(
        raw_kernel,
        [BLOCKS, ((HEAD_DIM, HALF), BF16), ((TOK + HEAD_DIM, HALF), F32), ((sharers, 4, TOK), F32)],
        queries, cotangent, gain, got, intra, chip, mine, received,
    )
    parts = over_heads(parts)
    total, own, other = call(
        grad_state_kernel,
        [PIECES, STATE, STATE],
        queries, cotangent, gain, got, raw, parts,
    )
    attended, grad_query, grad_kf, grad_vf, here, there = call(
        back_kernel,
        [WIDE_LOW, WIDE_LOW, WIDE, WIDE, STATE, PIECES],
        queries, key_input, value_input, cotangent, gain, raw, low, swap_cores(give), parts,
        own, other,
        flops=500_000_000,
    )
    (chip,) = scan(total, True)
    there = swap_cores(chip + there)
    parts = key_input, value_input, grad_kf, grad_vf
    own = call(own_kernel, [HALF_LOW, HALF_LOW], *parts, chip, here, flops=50_000_000)
    store = [pltpu.VMEM(*HALF_LOW)] * 2 + [pltpu.SemaphoreType.DMA((4,))]
    grad_key, grad_value = call(
        last_kernel,
        [WIDE_LOW, WIDE_LOW],
        *parts, there, *own,
        out_spaces=[pl.BlockSpec(memory_space=pltpu.HBM)] * 2,
        scratch=store,
    )
    return (attended, grad_query, grad_key, grad_value)


def solution(mesh):
    in_specs = (P("ctx", "head"), P("ctx", "head"), P("ctx", "head"), P("head"), P("ctx", "head"))
    out_specs = (P("ctx", "head"), P("ctx", "head"), P("ctx", "head"), P("ctx", "head"))
    return jax.shard_map(
        per_device, mesh=mesh, in_specs=in_specs, out_specs=out_specs, check_vma=False
    )
```

```python
import functools

import jax
import jax.numpy as jnp
from jax import lax
from jax.experimental import pallas as pl
from jax.experimental.pallas import tpu as pltpu
from jax.sharding import PartitionSpec as P

HEAD_DIM = 96
D = 6144
TOK = 128
LANES = 128
HALF_HEADS = 4
HALF = HALF_HEADS * HEAD_DIM
CHIPS = 64
CORES = 2
PIECE = 640
PARTS = 4
PART = CHIPS // PARTS

epsilon = 1e-06
F32 = jnp.float32
BF16 = jnp.bfloat16
VMEM = pl.BlockSpec(memory_space=pltpu.VMEM)
NN = (((1,), (0,)), ((), ()))
NT = (((1,), (1,)), ((), ()))
TN = (((0,), (0,)), ((), ()))


def mm(a, b, dims):
    return lax.dot_general(a, b, dims, preferred_element_type=F32)


def half(g):
    return slice(g * HALF, (g + 1) * HALF)


def head_masks(rows):
    lane = lax.broadcasted_iota(jnp.int32, (rows, HALF), 1)
    return [(lane >= h * HEAD_DIM) & (lane < (h + 1) * HEAD_DIM) for h in range(HALF_HEADS)]


def spread(x):
    return jnp.concatenate([x * m.astype(BF16) for m in head_masks(x.shape[0])], axis=0)


def diagonal(x):
    rows = x.shape[0] // HALF_HEADS
    masks = head_masks(rows)
    out = x[:rows]
    for h in range(1, HALF_HEADS):
        out = jnp.where(masks[h], x[h * rows : (h + 1) * rows], out)
    return out


def to_pieces(state):
    rest = state[64:96]
    tail = rest[:, 256:384]
    return jnp.concatenate(
        [
            state[0:64],
            jnp.concatenate([rest[:, 0:128], rest[:, 128:256]], axis=0),
            jnp.concatenate([tail, pltpu.roll(tail, 64, 1)], axis=0),
        ],
        axis=1,
    )


def from_pieces(pieces):
    low = lax.broadcasted_iota(jnp.int32, (32, LANES), 1) < 64
    tail = jnp.where(low, pieces[0:32, 512:640], pltpu.roll(pieces[32:64, 512:640], 64, 1))
    rest = jnp.concatenate([pieces[0:32, 384:512], pieces[32:64, 384:512], tail], axis=1)
    return jnp.concatenate([pieces[:, 0:384], rest], axis=0)


def silu_low(x):
    x = x.astype(F32)
    return (x * jax.nn.sigmoid(x)).astype(BF16)


def silu_slope(x):
    x = x.astype(F32)
    sig = jax.nn.sigmoid(x)
    return sig * (1.0 + x * (1.0 - sig))


def causal4():
    row = lax.broadcasted_iota(jnp.int32, (TOK, TOK), 0)
    col = lax.broadcasted_iota(jnp.int32, (TOK, TOK), 1)
    keep = jnp.where(row >= col, 1.0, 0.0)
    return jnp.concatenate([keep] * HALF_HEADS, axis=1) > 0.5


def by_head(x):
    return jnp.concatenate([x[:, h * TOK : (h + 1) * TOK] for h in range(HALF_HEADS)], axis=0)


def core_index():
    return lax.axis_index("ctx") % CORES


def pick(own, x):
    first = (core_index() == 0) == own
    return jnp.where(first, x[:, half(0)], x[:, half(1)])


def in_order(own, other):
    first = core_index() == 0
    return jnp.where(first, own, other), jnp.where(first, other, own)


def state_kernel(own, pair_ref, out_ref):
    k, v = pick(own, pair_ref[0]), pick(own, pair_ref[1])
    out_ref[:, 0, :] = to_pieces(diagonal(mm(silu_low(k), v, TN)))


def send_kernel(after_ref, q_ref, k_ref, v_ref, c_ref, qc_ref, kv_ref):
    for out_ref, refs in ((qc_ref, (q_ref, c_ref)), (kv_ref, (k_ref, v_ref))):
        for i, ref in enumerate(refs):
            out_ref[i] = pick(False, ref[...]).astype(F32)


def attention(q_feat, k_feat):
    return jnp.where(causal4(), mm(q_feat, spread(k_feat), NT), 0.0).astype(BF16)


def intra_kernel(q_ref, k_ref, v_ref, got_qc_ref, got_kv_ref, intra_ref):
    mine = [pick(True, ref[...]) for ref in (q_ref, k_ref, v_ref)]
    others = [x.astype(BF16) for x in (got_qc_ref[0], got_kv_ref[0], got_kv_ref[1])]
    for i, (q, k, v) in enumerate((mine, others)):
        intra_ref[i] = mm(attention(silu_low(q), silu_low(k)), spread(v), NN)


def scan_kernel(backward, pieces_ref, out_hbm, *refs):
    *done, rows_ref, sems = refs
    total = jnp.zeros((1, PIECE), F32)
    copies = []
    for part in range(PARTS):
        first = (PARTS - 1 - part if backward else part) * PART
        for i in range(PART):
            chip = first + (PART - 1 - i if backward else i)
            rows_ref[chip] = total
            total = total + pieces_ref[chip]
        rows = pl.ds(first, PART)
        copy = pltpu.make_async_copy(rows_ref.at[rows], out_hbm.at[rows], sems.at[part])
        copy.start()
        copies.append(copy)
    for ref in done:
        ref[...] = jnp.zeros_like(ref)
    for copy in copies:
        copy.wait()


def lane_sums(x):
    part = x[:, 0:LANES]
    for i in range(1, x.shape[1] // LANES):
        part = part + x[:, i * LANES : (i + 1) * LANES]
    return jnp.sum(part.T, axis=0, keepdims=True)


def raw_kernel(
    q_ref, c_ref, gain_ref, got_ref, intra_ref, chip_ref, mine_ref, received_ref,
    raw_ref, low_ref, give_ref, parts_ref,
):
    core = core_index()
    chip = chip_ref[:, 0, :]
    own = from_pieces(chip + jnp.where(core == 1, received_ref[:, 0, :], 0.0))
    other = from_pieces(chip + jnp.where(core == 0, mine_ref[:, 0, :], 0.0))
    low_ref[...] = own.astype(BF16)
    give_ref[TOK:, :] = other
    gain = pick(True, gain_ref[...])
    q, c = pick(True, q_ref[...]), pick(True, c_ref[...])
    sums = []
    for i, (q, c, state) in enumerate(
        ((q, c, own), (got_ref[0].astype(BF16), got_ref[1], other))
    ):
        raw = intra_ref[i] + mm(silu_low(q), spread(state.astype(BF16)), NN)
        raw_ref[i] = raw
        upstream = c.astype(F32) * gain
        sums.append(jnp.concatenate([lane_sums(raw * raw), lane_sums(upstream * raw)], axis=0))
    give_ref[0:TOK, :] = raw_ref[1]
    sums = jnp.concatenate(in_order(*sums), axis=0)
    parts_ref[...] = jnp.broadcast_to(sums[None], parts_ref.shape)


def scales(totals):
    square = jnp.broadcast_to(totals[0:1], (TOK, LANES)).T
    cross = jnp.broadcast_to(totals[1:2], (TOK, LANES)).T
    mean = square * (1.0 / D) + epsilon
    pair = lax.rsqrt(mean), cross / (D * mean)
    return [jnp.concatenate([x] * (HALF // LANES), axis=1) for x in pair]


def gradient(c, gain, raw, inverse, pull):
    return ((c.astype(F32) * gain - raw * pull) * inverse).astype(BF16)


def own_and_other(parts_ref):
    totals = jnp.sum(parts_ref[...], axis=0)
    return in_order(totals[0:2], totals[2:4])


def grad_state_kernel(
    q_ref, c_ref, gain_ref, got_ref, raw_ref, parts_ref, sum_ref, late_q_ref, late_d_ref
):
    gain = pick(True, gain_ref[...])
    q, c = pick(True, q_ref[...]), pick(True, c_ref[...])
    features, gradients = [], []
    for i, (q, c, totals) in enumerate(
        zip((q, got_ref[0].astype(BF16)), (c, got_ref[1]), own_and_other(parts_ref))
    ):
        features.append(silu_low(q))
        gradients.append(gradient(c, gain, raw_ref[i], *scales(totals)))
    late_q_ref[...] = in_order(*features)[1]
    late_d_ref[...] = in_order(*gradients)[1]
    both = [jnp.concatenate(x, axis=0) for x in (features, gradients)]
    sum_ref[:, 0, :] = to_pieces(diagonal(mm(*both, TN)))


def back_kernel(
    q_ref, k_ref, v_ref, c_ref, gain_ref, raw_ref, low_ref, got_ref, parts_ref, late_q_ref, late_d_ref,
    attended_ref, grad_q_ref, grad_kf_ref, grad_vf_ref, here_ref, there_ref,
):
    core = core_index()
    late = diagonal(mm(late_q_ref[...], late_d_ref[...], TN))
    here_ref[...] = jnp.where(core == 0, late, 0.0)
    there_ref[:, 0, :] = to_pieces(jnp.where(core == 1, late, 0.0))
    keep = causal4()
    inverse, pull = scales(own_and_other(parts_ref)[0])
    raws = in_order(raw_ref[0], got_ref[0:TOK])
    lows = in_order(low_ref[...].astype(F32), got_ref[TOK:])
    for g in range(CORES):
        q, raw, gain = q_ref[:, half(g)], raws[g], gain_ref[:, half(g)]
        q_feat, k_feat = silu_low(q), silu_low(k_ref[:, half(g)])
        attended_ref[:, half(g)] = (raw * inverse * gain).astype(BF16)
        d_raw = gradient(c_ref[:, half(g)], gain, raw, inverse, pull)
        back = jnp.where(keep, mm(d_raw, spread(v_ref[:, half(g)]), NT), 0.0).astype(BF16)
        grad_qf = mm(back, spread(k_feat), NN) + mm(d_raw, spread(lows[g].astype(BF16)), NT)
        grad_q_ref[:, half(g)] = (grad_qf * silu_slope(q)).astype(BF16)
        grad_kf_ref[:, half(g)] = mm(by_head(back), spread(q_feat), TN)
        grad_vf_ref[:, half(g)] = mm(by_head(attention(q_feat, k_feat)), spread(d_raw), TN)


def finished(own, refs, later):
    k, v, grad_kf, grad_vf = (pick(own, ref[...]) for ref in refs)
    later = spread(later.astype(BF16))
    grad_k = (grad_kf + mm(v, later, NT)) * silu_slope(k)
    return grad_k.astype(BF16), (grad_vf + mm(silu_low(k), later, NN)).astype(BF16)


def own_kernel(
    k_ref, v_ref, grad_kf_ref, grad_vf_ref, chip_ref, here_ref, grad_k_ref, grad_v_ref
):
    later = from_pieces(chip_ref[:, 0, :]) + here_ref[...]
    refs = k_ref, v_ref, grad_kf_ref, grad_vf_ref
    grad_k_ref[...], grad_v_ref[...] = finished(True, refs, later)


def last_kernel(
    k_ref, v_ref, grad_kf_ref, grad_vf_ref, there_ref, own_k_ref, own_v_ref,
    grad_k_hbm, grad_v_hbm, other_k_ref, other_v_ref, sems,
):
    core = core_index()
    own = pl.ds(pl.multiple_of(core * HALF, HALF), HALF)
    other = pl.ds(pl.multiple_of((1 - core) * HALF, HALF), HALF)
    copies = [
        pltpu.make_async_copy(own_k_ref, grad_k_hbm.at[:, own], sems.at[0]),
        pltpu.make_async_copy(own_v_ref, grad_v_hbm.at[:, own], sems.at[1]),
        pltpu.make_async_copy(other_k_ref, grad_k_hbm.at[:, other], sems.at[2]),
        pltpu.make_async_copy(other_v_ref, grad_v_hbm.at[:, other], sems.at[3]),
    ]
    copies[0].start()
    copies[1].start()
    refs = k_ref, v_ref, grad_kf_ref, grad_vf_ref
    later = from_pieces(there_ref[:, 0, :])
    other_k_ref[...], other_v_ref[...] = finished(False, refs, later)
    copies[2].start()
    copies[3].start()
    for copy in copies:
        copy.wait()


def call(kernel, outs, *args, flops=0, out_spaces=None, scratch=()):
    return pl.pallas_call(
        kernel,
        out_shape=[jax.ShapeDtypeStruct(shape, kind) for shape, kind in outs],
        in_specs=[VMEM] * len(args),
        out_specs=out_spaces or [VMEM] * len(outs),
        scratch_shapes=list(scratch),
        compiler_params=pltpu.CompilerParams(vmem_limit_bytes=32 * 1024 * 1024),
        cost_estimate=pl.CostEstimate(flops=flops, bytes_accessed=1_000_000, transcendentals=0),
    )(*args)


def swap_cores(x):
    pairs = [(i, i ^ 1) for i in range(CHIPS * CORES)]
    return lax.ppermute(x, "ctx", pairs)


def across_chips(x):
    groups = [[chip * CORES + core for chip in range(CHIPS)] for core in range(CORES)]
    return lax.all_to_all(x, "ctx", 0, 0, axis_index_groups=groups)


def over_heads(x):
    size = CORES * lax.axis_size("head")
    groups = [[chip * size + i for i in range(size)] for chip in range(CHIPS)]
    return lax.all_to_all(x, ("ctx", "head"), 0, 0, axis_index_groups=groups)


PIECES = ((CHIPS, 1, PIECE), F32)
WIDE = ((TOK, CORES * HALF), F32)
WIDE_LOW = ((TOK, CORES * HALF), BF16)
STATE = ((HEAD_DIM, HALF), F32)
HALF_LOW = ((TOK, HALF), BF16)
BLOCKS = ((CORES, TOK, HALF), F32)


def scan(pieces, backward):
    def kernel(*refs):
        scan_kernel(backward, *refs)

    done = [] if backward else [((8, LANES), F32)]
    spaces = [pl.BlockSpec(memory_space=pltpu.HBM)] + [VMEM] * len(done)
    rows = [pltpu.VMEM(*PIECES), pltpu.SemaphoreType.DMA((PARTS,))]
    summed, *done = call(
        kernel, [PIECES] + done, across_chips(pieces), out_spaces=spaces, scratch=rows
    )
    return across_chips(summed), *done


def per_device(queries, key_input, value_input, norm_gain, cotangent):
    sharers = CORES * lax.axis_size("head")
    gain = norm_gain.reshape(1, -1)
    pair = jnp.stack([key_input, value_input])
    (theirs,) = call(functools.partial(state_kernel, False), [PIECES], pair)
    received = swap_cores(theirs)
    (mine,) = call(functools.partial(state_kernel, True), [PIECES], pair)
    chip, done = scan(mine + received, False)
    halves = call(
        send_kernel,
        [((2, TOK, HALF), F32)] * 2,
        done, queries, key_input, value_input, cotangent,
    )
    got, got_kv = (swap_cores(x) for x in halves)
    (intra,) = call(
        intra_kernel,
        [BLOCKS],
        queries, key_input, value_input, got, got_kv,
        flops=200_000_000,
    )
    raw, low, give, parts = call(
        raw_kernel,
        [BLOCKS, ((HEAD_DIM, HALF), BF16), ((TOK + HEAD_DIM, HALF), F32), ((sharers, 4, TOK), F32)],
        queries, cotangent, gain, got, intra, chip, mine, received,
    )
    parts = over_heads(parts)
    total, late_q, late_d = call(
        grad_state_kernel,
        [PIECES, HALF_LOW, HALF_LOW],
        queries, cotangent, gain, got, raw, parts,
    )
    attended, grad_query, grad_kf, grad_vf, here, there = call(
        back_kernel,
        [WIDE_LOW, WIDE_LOW, WIDE, WIDE, STATE, PIECES],
        queries, key_input, value_input, cotangent, gain, raw, low, swap_cores(give), parts,
        late_q, late_d,
        flops=500_000_000,
    )
    (chip,) = scan(total, True)
    there = swap_cores(chip + there)
    parts = key_input, value_input, grad_kf, grad_vf
    own = call(own_kernel, [HALF_LOW, HALF_LOW], *parts, chip, here, flops=50_000_000)
    store = [pltpu.VMEM(*HALF_LOW)] * 2 + [pltpu.SemaphoreType.DMA((4,))]
    grad_key, grad_value = call(
        last_kernel,
        [WIDE_LOW, WIDE_LOW],
        *parts, there, *own,
        out_spaces=[pl.BlockSpec(memory_space=pltpu.HBM)] * 2,
        scratch=store,
    )
    return (attended, grad_query, grad_key, grad_value)


def solution(mesh):
    in_specs = (P("ctx", "head"), P("ctx", "head"), P("ctx", "head"), P("head"), P("ctx", "head"))
    out_specs = (P("ctx", "head"), P("ctx", "head"), P("ctx", "head"), P("ctx", "head"))
    return jax.shard_map(
        per_device, mesh=mesh, in_specs=in_specs, out_specs=out_specs, check_vma=False
    )
```

```python
import functools

import jax
import jax.numpy as jnp
from jax import lax
from jax.experimental import pallas as pl
from jax.experimental.pallas import tpu as pltpu
from jax.sharding import PartitionSpec as P

HEAD_DIM = 96
D = 6144
TOK = 128
LANES = 128
HALF_HEADS = 4
HALF = HALF_HEADS * HEAD_DIM
CHIPS = 64
CORES = 2
PIECE = 640
PARTS = 4
PART = CHIPS // PARTS

epsilon = 1e-06
F32 = jnp.float32
BF16 = jnp.bfloat16
VMEM = pl.BlockSpec(memory_space=pltpu.VMEM)
NN = (((1,), (0,)), ((), ()))
NT = (((1,), (1,)), ((), ()))
TN = (((0,), (0,)), ((), ()))


def mm(a, b, dims):
    return lax.dot_general(a, b, dims, preferred_element_type=F32)


def half(g):
    return slice(g * HALF, (g + 1) * HALF)


def head_masks(rows):
    lane = lax.broadcasted_iota(jnp.int32, (rows, HALF), 1)
    return [(lane >= h * HEAD_DIM) & (lane < (h + 1) * HEAD_DIM) for h in range(HALF_HEADS)]


def spread(x):
    return jnp.concatenate([x * m.astype(BF16) for m in head_masks(x.shape[0])], axis=0)


def diagonal(x):
    rows = x.shape[0] // HALF_HEADS
    masks = head_masks(rows)
    out = x[:rows]
    for h in range(1, HALF_HEADS):
        out = jnp.where(masks[h], x[h * rows : (h + 1) * rows], out)
    return out


def to_pieces(state):
    rest = state[64:96]
    tail = rest[:, 256:384]
    return jnp.concatenate(
        [
            state[0:64],
            jnp.concatenate([rest[:, 0:128], rest[:, 128:256]], axis=0),
            jnp.concatenate([tail, pltpu.roll(tail, 64, 1)], axis=0),
        ],
        axis=1,
    )


def from_pieces(pieces):
    low = lax.broadcasted_iota(jnp.int32, (32, LANES), 1) < 64
    tail = jnp.where(low, pieces[0:32, 512:640], pltpu.roll(pieces[32:64, 512:640], 64, 1))
    rest = jnp.concatenate([pieces[0:32, 384:512], pieces[32:64, 384:512], tail], axis=1)
    return jnp.concatenate([pieces[:, 0:384], rest], axis=0)


def silu_low(x):
    x = x.astype(F32)
    return (x * jax.nn.sigmoid(x)).astype(BF16)


def silu_slope(x):
    x = x.astype(F32)
    sig = jax.nn.sigmoid(x)
    return sig * (1.0 + x * (1.0 - sig))


def causal4():
    row = lax.broadcasted_iota(jnp.int32, (TOK, TOK), 0)
    col = lax.broadcasted_iota(jnp.int32, (TOK, TOK), 1)
    keep = jnp.where(row >= col, 1.0, 0.0)
    return jnp.concatenate([keep] * HALF_HEADS, axis=1) > 0.5


def by_head(x):
    return jnp.concatenate([x[:, h * TOK : (h + 1) * TOK] for h in range(HALF_HEADS)], axis=0)


def core_index():
    return lax.axis_index("ctx") % CORES


def pick(own, x):
    first = (core_index() == 0) == own
    return jnp.where(first, x[:, half(0)], x[:, half(1)])


def in_order(own, other):
    first = core_index() == 0
    return jnp.where(first, own, other), jnp.where(first, other, own)


def state_kernel(own, pair_ref, out_ref):
    k, v = pick(own, pair_ref[0]), pick(own, pair_ref[1])
    out_ref[:, 0, :] = to_pieces(diagonal(mm(silu_low(k), v, TN)))


def send_kernel(after_ref, q_ref, k_ref, v_ref, c_ref, qc_ref, kv_ref):
    for out_ref, refs in ((qc_ref, (q_ref, c_ref)), (kv_ref, (k_ref, v_ref))):
        for i, ref in enumerate(refs):
            out_ref[i] = pick(False, ref[...]).astype(F32)


def attention(q_feat, k_feat):
    return jnp.where(causal4(), mm(q_feat, spread(k_feat), NT), 0.0).astype(BF16)


def intra_kernel(q_ref, k_ref, v_ref, got_qc_ref, got_kv_ref, intra_ref):
    mine = [pick(True, ref[...]) for ref in (q_ref, k_ref, v_ref)]
    others = [x.astype(BF16) for x in (got_qc_ref[0], got_kv_ref[0], got_kv_ref[1])]
    for i, (q, k, v) in enumerate((mine, others)):
        intra_ref[i] = mm(attention(silu_low(q), silu_low(k)), spread(v), NN)


def scan_kernel(backward, pieces_ref, out_hbm, *refs):
    *done, rows_ref, sems = refs
    total = jnp.zeros((1, PIECE), F32)
    copies = []
    for part in range(PARTS):
        first = (PARTS - 1 - part if backward else part) * PART
        for i in range(PART):
            chip = first + (PART - 1 - i if backward else i)
            rows_ref[chip] = total
            total = total + pieces_ref[chip]
        rows = pl.ds(first, PART)
        copy = pltpu.make_async_copy(rows_ref.at[rows], out_hbm.at[rows], sems.at[part])
        copy.start()
        copies.append(copy)
    for ref in done:
        ref[...] = jnp.zeros_like(ref)
    for copy in copies:
        copy.wait()


def lane_sums(x):
    part = x[:, 0:LANES]
    for i in range(1, x.shape[1] // LANES):
        part = part + x[:, i * LANES : (i + 1) * LANES]
    return jnp.sum(part.T, axis=0, keepdims=True)


def raw_kernel(
    q_ref, c_ref, gain_ref, got_ref, intra_ref, chip_ref, mine_ref, received_ref,
    raw_ref, low_ref, give_ref, parts_ref,
):
    core = core_index()
    chip = chip_ref[:, 0, :]
    own = from_pieces(chip + jnp.where(core == 1, received_ref[:, 0, :], 0.0))
    other = from_pieces(chip + jnp.where(core == 0, mine_ref[:, 0, :], 0.0))
    low_ref[...] = own.astype(BF16)
    give_ref[TOK:, :] = other
    gain = pick(True, gain_ref[...])
    q, c = pick(True, q_ref[...]), pick(True, c_ref[...])
    sums = []
    for i, (q, c, state) in enumerate(
        ((q, c, own), (got_ref[0].astype(BF16), got_ref[1], other))
    ):
        raw = intra_ref[i] + mm(silu_low(q), spread(state.astype(BF16)), NN)
        raw_ref[i] = raw
        upstream = c.astype(F32) * gain
        sums.append(jnp.concatenate([lane_sums(raw * raw), lane_sums(upstream * raw)], axis=0))
    give_ref[0:TOK, :] = raw_ref[1]
    sums = jnp.concatenate(in_order(*sums), axis=0)
    parts_ref[...] = jnp.broadcast_to(sums[None], parts_ref.shape)


def scales(totals):
    square = jnp.broadcast_to(totals[0:1], (TOK, LANES)).T
    cross = jnp.broadcast_to(totals[1:2], (TOK, LANES)).T
    mean = square * (1.0 / D) + epsilon
    pair = lax.rsqrt(mean), cross / (D * mean)
    return [jnp.concatenate([x] * (HALF // LANES), axis=1) for x in pair]


def gradient(c, gain, raw, inverse, pull):
    return ((c.astype(F32) * gain - raw * pull) * inverse).astype(BF16)


def own_and_other(parts_ref):
    totals = jnp.sum(parts_ref[...], axis=0)
    return in_order(totals[0:2], totals[2:4])


def grad_state_kernel(
    q_ref, c_ref, gain_ref, got_ref, raw_ref, parts_ref, sum_ref, own_ref, other_ref
):
    gain = pick(True, gain_ref[...])
    q, c = pick(True, q_ref[...]), pick(True, c_ref[...])
    states = []
    for i, (q, c, totals) in enumerate(
        zip((q, got_ref[0].astype(BF16)), (c, got_ref[1]), own_and_other(parts_ref))
    ):
        d_raw = gradient(c, gain, raw_ref[i], *scales(totals))
        states.append(diagonal(mm(silu_low(q), d_raw, TN)))
    own_ref[...], other_ref[...] = states
    sum_ref[:, 0, :] = to_pieces(states[0] + states[1])


def back_kernel(
    q_ref, k_ref, v_ref, c_ref, gain_ref, raw_ref, low_ref, got_ref, parts_ref, own_ref, other_ref,
    attended_ref, grad_q_ref, grad_kf_ref, grad_vf_ref, here_ref, there_ref,
):
    core = core_index()
    here_ref[...] = jnp.where(core == 0, other_ref[...], 0.0)
    there_ref[:, 0, :] = to_pieces(jnp.where(core == 1, own_ref[...], 0.0))
    keep = causal4()
    inverse, pull = scales(own_and_other(parts_ref)[0])
    raws = in_order(raw_ref[0], got_ref[0:TOK])
    lows = in_order(low_ref[...].astype(F32), got_ref[TOK:])
    for g in range(CORES):
        q, raw, gain = q_ref[:, half(g)], raws[g], gain_ref[:, half(g)]
        q_feat, k_feat = silu_low(q), silu_low(k_ref[:, half(g)])
        attended_ref[:, half(g)] = (raw * inverse * gain).astype(BF16)
        d_raw = gradient(c_ref[:, half(g)], gain, raw, inverse, pull)
        back = jnp.where(keep, mm(d_raw, spread(v_ref[:, half(g)]), NT), 0.0).astype(BF16)
        grad_qf = mm(back, spread(k_feat), NN) + mm(d_raw, spread(lows[g].astype(BF16)), NT)
        grad_q_ref[:, half(g)] = (grad_qf * silu_slope(q)).astype(BF16)
        grad_kf_ref[:, half(g)] = mm(by_head(back), spread(q_feat), TN)
        grad_vf_ref[:, half(g)] = mm(by_head(attention(q_feat, k_feat)), spread(d_raw), TN)


def finished(own, refs, later):
    k, v, grad_kf, grad_vf = (pick(own, ref[...]) for ref in refs)
    later = spread(later.astype(BF16))
    grad_k = (grad_kf + mm(v, later, NT)) * silu_slope(k)
    return grad_k.astype(BF16), (grad_vf + mm(silu_low(k), later, NN)).astype(BF16)


def own_kernel(
    k_ref, v_ref, grad_kf_ref, grad_vf_ref, chip_ref, here_ref, grad_k_ref, grad_v_ref
):
    later = from_pieces(chip_ref[:, 0, :]) + here_ref[...]
    refs = k_ref, v_ref, grad_kf_ref, grad_vf_ref
    grad_k_ref[...], grad_v_ref[...] = finished(True, refs, later)


def last_kernel(
    k_ref, v_ref, grad_kf_ref, grad_vf_ref, there_ref, own_k_ref, own_v_ref,
    grad_k_hbm, grad_v_hbm, other_k_ref, other_v_ref, sems,
):
    core = core_index()
    own = pl.ds(pl.multiple_of(core * HALF, HALF), HALF)
    other = pl.ds(pl.multiple_of((1 - core) * HALF, HALF), HALF)
    copies = [
        pltpu.make_async_copy(own_k_ref, grad_k_hbm.at[:, own], sems.at[0]),
        pltpu.make_async_copy(own_v_ref, grad_v_hbm.at[:, own], sems.at[1]),
        pltpu.make_async_copy(other_k_ref, grad_k_hbm.at[:, other], sems.at[2]),
        pltpu.make_async_copy(other_v_ref, grad_v_hbm.at[:, other], sems.at[3]),
    ]
    copies[0].start()
    copies[1].start()
    refs = k_ref, v_ref, grad_kf_ref, grad_vf_ref
    later = from_pieces(there_ref[:, 0, :])
    other_k_ref[...], other_v_ref[...] = finished(False, refs, later)
    copies[2].start()
    copies[3].start()
    for copy in copies:
        copy.wait()


def call(kernel, outs, *args, flops=0, out_spaces=None, scratch=()):
    return pl.pallas_call(
        kernel,
        out_shape=[jax.ShapeDtypeStruct(shape, kind) for shape, kind in outs],
        in_specs=[VMEM] * len(args),
        out_specs=out_spaces or [VMEM] * len(outs),
        scratch_shapes=list(scratch),
        compiler_params=pltpu.CompilerParams(vmem_limit_bytes=32 * 1024 * 1024),
        cost_estimate=pl.CostEstimate(flops=flops, bytes_accessed=1_000_000, transcendentals=0),
    )(*args)


def swap_cores(x):
    pairs = [(i, i ^ 1) for i in range(CHIPS * CORES)]
    return lax.ppermute(x, "ctx", pairs)


def across_chips(x):
    groups = [[chip * CORES + core for chip in range(CHIPS)] for core in range(CORES)]
    return lax.all_to_all(x, "ctx", 0, 0, axis_index_groups=groups)


def over_heads(x):
    size = lax.axis_size("head")
    groups = [
        [(chip * CORES + core) * size + i for i in range(size) for core in range(CORES)]
        for chip in range(CHIPS)
    ]
    return lax.all_to_all(x, ("ctx", "head"), 0, 0, axis_index_groups=groups)


PIECES = ((CHIPS, 1, PIECE), F32)
WIDE = ((TOK, CORES * HALF), F32)
WIDE_LOW = ((TOK, CORES * HALF), BF16)
STATE = ((HEAD_DIM, HALF), F32)
HALF_LOW = ((TOK, HALF), BF16)
BLOCKS = ((CORES, TOK, HALF), F32)


def scan(pieces, backward):
    def kernel(*refs):
        scan_kernel(backward, *refs)

    done = [] if backward else [((8, LANES), F32)]
    spaces = [pl.BlockSpec(memory_space=pltpu.HBM)] + [VMEM] * len(done)
    rows = [pltpu.VMEM(*PIECES), pltpu.SemaphoreType.DMA((PARTS,))]
    summed, *done = call(
        kernel, [PIECES] + done, across_chips(pieces), out_spaces=spaces, scratch=rows
    )
    return across_chips(summed), *done


def per_device(queries, key_input, value_input, norm_gain, cotangent):
    sharers = CORES * lax.axis_size("head")
    gain = norm_gain.reshape(1, -1)
    pair = jnp.stack([key_input, value_input])
    (theirs,) = call(functools.partial(state_kernel, False), [PIECES], pair)
    received = swap_cores(theirs)
    (mine,) = call(functools.partial(state_kernel, True), [PIECES], pair)
    chip, done = scan(mine + received, False)
    halves = call(
        send_kernel,
        [((2, TOK, HALF), F32)] * 2,
        done, queries, key_input, value_input, cotangent,
    )
    got, got_kv = (swap_cores(x) for x in halves)
    (intra,) = call(
        intra_kernel,
        [BLOCKS],
        queries, key_input, value_input, got, got_kv,
        flops=200_000_000,
    )
    raw, low, give, parts = call(
        raw_kernel,
        [BLOCKS, ((HEAD_DIM, HALF), BF16), ((TOK + HEAD_DIM, HALF), F32), ((sharers, 4, TOK), F32)],
        queries, cotangent, gain, got, intra, chip, mine, received,
    )
    parts = over_heads(parts)
    total, own, other = call(
        grad_state_kernel,
        [PIECES, STATE, STATE],
        queries, cotangent, gain, got, raw, parts,
    )
    attended, grad_query, grad_kf, grad_vf, here, there = call(
        back_kernel,
        [WIDE_LOW, WIDE_LOW, WIDE, WIDE, STATE, PIECES],
        queries, key_input, value_input, cotangent, gain, raw, low, swap_cores(give), parts,
        own, other,
        flops=500_000_000,
    )
    (chip,) = scan(total, True)
    there = swap_cores(chip + there)
    parts = key_input, value_input, grad_kf, grad_vf
    own = call(own_kernel, [HALF_LOW, HALF_LOW], *parts, chip, here, flops=50_000_000)
    store = [pltpu.VMEM(*HALF_LOW)] * 2 + [pltpu.SemaphoreType.DMA((4,))]
    grad_key, grad_value = call(
        last_kernel,
        [WIDE_LOW, WIDE_LOW],
        *parts, there, *own,
        out_spaces=[pl.BlockSpec(memory_space=pltpu.HBM)] * 2,
        scratch=store,
    )
    return (attended, grad_query, grad_key, grad_value)


def solution(mesh):
    in_specs = (P("ctx", "head"), P("ctx", "head"), P("ctx", "head"), P("head"), P("ctx", "head"))
    out_specs = (P("ctx", "head"), P("ctx", "head"), P("ctx", "head"), P("ctx", "head"))
    return jax.shard_map(
        per_device, mesh=mesh, in_specs=in_specs, out_specs=out_specs, check_vma=False
    )
```
